256 devices in a mesh: row: 8 (over y, core), col: 32 (over x, z).
Axes of the slice: x: 4, y: 4, z: 8, core: 2. Of those that a mesh axis runs over, the one named last changes fastest.
Arguments:
- radial: bfloat16 [640, 48, 1024], P('col', None, 'row'), may hold values from -1 to 1
- form_factors: float32 [256, 1024], replicated, may hold values from -6 to 6
- coupling: int32 [320, 640], P('row', 'col'), may hold values from 0 to 15
- quantum: int32 [640, 3], replicated, may hold values from 0 to 3
- green_diag: float32 [640, 48], P('col'), may hold values from -0.1 to 0.1
- kmatrix: bfloat16 [30720, 128], P('col'), may hold values from -6 to 6
- born_term: float32 [15360, 128], P('row'), may hold values from -3 to 3
Outputs:
- v_block: bfloat16 [15360, 30720], P('row', 'col')
- first_iterate: bfloat16 [15360, 128], P('row')
- second_iterate: float32 [15360, 128], P('row', 'col')
The draws below stay inside these ranges and needn't reach their ends.
All inputs are finite; a program needn't handle non-finite values.
Results may differ from the reference program's by a relative error of at most 0.008.
Values may be sent and summed in bfloat16 or wider, within the bound.
A program may use at most 128 MiB of HBM per device.

```python
import jax
import jax.numpy as jnp
from jax import lax

NK = 48
R = 1024
NOS = 128
NLAM = 16
NTARG = 4
NCH = 640
SLAB = 320
NF = 256


def set_ends(result, own_key, smallest, high):
    longest = result.shape.index(max(result.shape))
    spots = []
    for shift in (0, 1):
        where = [jax.random.randint(jax.random.fold_in(own_key, axis), (), 0, length) for axis, length in enumerate(result.shape)]
        where[longest] = (where[longest] + shift) % result.shape[longest]
        spots.append(tuple(where))
    return result.at[spots[0]].set(smallest).at[spots[1]].set(high)


def block_scale(rng, extent, split, smallest, largest):
    factor_of = 1.0
    for axis_at, blocks in split:
        draws = jax.random.uniform(jax.random.fold_in(jax.random.fold_in(rng, 6), axis_at), (blocks,), jnp.float32, smallest / len(split), largest / len(split))
        factor_of = factor_of * jnp.repeat(jnp.exp(draws), extent[axis_at] // blocks).reshape((-1,) + (1,) * (len(extent) - 1 - axis_at))
    return factor_of


def scatter_about(stream_key, dims, spread, limit, shards=(), held_as=jnp.bfloat16):
    entries = spread * jax.random.normal(stream_key, dims, jnp.float32)
    if shards:
        entries = entries * block_scale(stream_key, dims, shards, -0.22, 0.18)
    return jnp.clip(entries, -limit, limit).astype(held_as)


def setup_inputs(seed: int = 0) -> dict:
    key_of = jax.random.split(jax.random.key(seed), 8)
    return {
        "radial": scatter_about(key_of[0], (NCH, NK, R), 0.18, 1.0, ((0, 32), (2, 8))),
        "form_factors": scatter_about(key_of[1], (NF, R), 1.0, 6.0, (), jnp.float32),
        "coupling": set_ends(jax.random.randint(key_of[2], (SLAB, NCH), 0, NLAM), jax.random.fold_in(key_of[2], 1), 0, NLAM - 1).astype(jnp.int32),
        "quantum": set_ends(jax.random.randint(key_of[3], (NCH, 3), 0, NTARG), jax.random.fold_in(key_of[3], 1), 0, NTARG - 1).astype(jnp.int32),
        "green_diag": jnp.clip(jax.random.uniform(key_of[4], (NCH, NK), jnp.float32, -0.1, 0.1) * block_scale(key_of[4], (NCH, NK), ((0, 32),), -0.4, 0.0), -0.1, 0.1),
        "kmatrix": scatter_about(key_of[5], (NCH * NK, NOS), 1.0, 6.0, ((0, 32),)),
        "born_term": scatter_about(key_of[6], (SLAB * NK, NOS), 0.5, 3.0, ((0, 8),), jnp.float32),
    }


def reference(radial, form_factors, coupling, quantum, green_diag, kmatrix, born_term):
    slab_quant = quantum[:SLAB]
    table_index = coupling * (NTARG * NTARG) + slab_quant[:, 2:3] * NTARG + quantum[:, 2][None, :]
    parity = (slab_quant[:, 0:1] + quantum[:, 0][None, :]) % 2
    spread_m = jnp.abs(slab_quant[:, 1:2] - quantum[:, 1][None, :])
    angular = (1.0 - 2.0 * parity.astype(jnp.float32)) / (1.0 + spread_m.astype(jnp.float32))
    radial_wide = radial.astype(jnp.float32)

    def one_channel(operands):
        channel_rows, index_row, angle_row = operands
        weights = form_factors[index_row] * angle_row[:, None]
        scaled = (radial_wide * weights[:, None, :]).astype(jnp.bfloat16)
        return jnp.einsum("kr,bqr->kbq", channel_rows.astype(jnp.float32), scaled.astype(jnp.float32)).astype(jnp.bfloat16)

    blocks = lax.map(one_channel, (radial[:SLAB], table_index, angular))
    v_block = blocks.reshape(SLAB * NK, NCH * NK)
    green_flat = green_diag.reshape(-1, 1)
    weighted = (green_flat * kmatrix.astype(jnp.float32)).astype(jnp.bfloat16)
    first_iterate = (born_term + jnp.dot(v_block, weighted, preferred_element_type=jnp.float32)).astype(jnp.bfloat16)
    updated = jnp.concatenate([first_iterate, kmatrix[SLAB * NK:]], axis=0)
    weighted_next = (green_flat * updated.astype(jnp.float32)).astype(jnp.bfloat16)
    second_iterate = born_term + jnp.dot(v_block, weighted_next, preferred_element_type=jnp.float32)
    return v_block, first_iterate, second_iterate
```

```python
import functools

import jax
import jax.numpy as jnp
from jax import lax
from jax.experimental import pallas as pl
from jax.experimental.pallas import tpu as pltpu
from jax.sharding import PartitionSpec as P

NTARG = 4
MESH = pl.DeviceIdType.MESH
BF, F32 = jnp.bfloat16, jnp.float32

NX, NZ, NY = 4, 8, 4
NROW = 8
MOM = 48
GRID = 1024
LANE = 128
NB = 20
GRP = 10
HALF = 5
HROW = HALF * MOM
GROW = GRP * MOM
COLS = NB * MOM
ROWS = 4 * GROW
SH = 64
WIN = 4
NWIN = NB // WIN


def kernel(idx_ref, ang_ref, rad_ref, form_ref, gb_ref, kmat_ref, born_ref,
           v_out, first_out, share_out,
           table, colp, rowp, vbuf, weighted, pown, psend, precv, ssum, zsend, zrecv, bornp,
           fi, upd, t32, t16, pbuf, txrecv, tz32, tzsend, tzrecv,
           sc_s, sc_r, y_s, y_r, z_s, z_r, x_s, x_r, p_s, p_r, r_s, r_r, u_s, u_r,
           fz_s, fz_r, fx_s, fx_r, tx_s, tx_r, tz_s, tz_r, out_s):
    row = lax.axis_index("row")
    col = lax.axis_index("col")
    x, z = col // NZ, col % NZ
    y, core = row // 2, row % 2

    def at_x(d):
        return (row, lax.rem(x + d, NX) * NZ + z)

    def at_z(d):
        return (row, x * NZ + lax.rem(z + d, NZ))

    def at_y(d):
        return (lax.rem(y + d, NY) * 2 + core, col)

    sibling = (y * 2 + 1 - core, col)
    in_slab = col < 2 * NROW
    panel_row, part = col // 2, col % 2

    def scatter_to(h):
        return (panel_row, (2 * part + h) * NZ + row)

    def scatter_self(h):
        return (panel_row == row) & ((2 * part + h) * NZ + row == col)

    use_col = 2 * row + x // 2
    use_self = use_col == col
    source_self = (col // 2 == row) & (x // 2 == part)

    def copy(src, dst, ss, rs, dev):
        return pltpu.make_async_remote_copy(src_ref=src, dst_ref=dst, send_sem=ss, recv_sem=rs,
                                            device_id=dev, device_id_type=MESH)

    bar = pltpu.get_barrier_semaphore()

    def greet(dev):
        pl.semaphore_signal(bar, inc=1, device_id=dev, device_id_type=MESH)

    for d in range(1, NZ):
        greet(at_z(d))
    for d in range(1, NX):
        greet(at_x(d))
    greet(at_y(1))
    greet(at_y(3))
    greet(sibling)
    sc_src_row, sc_src_col = z, 2 * row + x // 2
    sc_from_self = (sc_src_row == row) & (sc_src_col == col)

    @pl.when(jnp.logical_not(sc_from_self))
    def _():
        greet((sc_src_row, sc_src_col))

    @pl.when(in_slab)
    def _():
        def hello(k, carry):
            g, zz = 2 * part + k // NZ, lax.rem(k, NZ)
            me = (panel_row == row) & (g * NZ + zz == col)

            @pl.when(jnp.logical_not(me))
            def _():
                greet((panel_row, g * NZ + zz))
            return carry

        lax.fori_loop(0, 2 * NZ, hello, 0)

    colp[:, COLS:, :] = jnp.zeros((NROW, 1024 - COLS, LANE), BF)
    zsend[GROW:, :] = jnp.zeros((NZ * SH - GROW, LANE), BF)
    ssum[GROW:, :] = jnp.zeros((NZ * SH - GROW, LANE), F32)
    bornp[GROW:, :] = jnp.zeros((NZ * SH - GROW, LANE), F32)
    t32[:, 60:, :] = jnp.zeros((NX * NZ, 4, LANE), F32)

    n_wait = 7 + 3 + 3 + 8 - use_self.astype(jnp.int32)
    n_wait = n_wait + jnp.where(in_slab, 2 - scatter_self(0).astype(jnp.int32) - scatter_self(1).astype(jnp.int32), 0)
    pl.semaphore_wait(bar, n_wait)

    def sc_copy(h, half):
        p = 2 * h + half
        return copy(rad_ref.at[pl.ds(p * HROW, HROW)], rowp.at[2 * part + h, half, row], sc_s.at[p], sc_r.at[half],
                    scatter_to(h))

    for half in range(2):
        for h in range(2):
            @pl.when(in_slab & jnp.logical_not(scatter_self(h)))
            def _():
                sc_copy(h, half).start()

            @pl.when(in_slab & scatter_self(h))
            def _():
                rowp[2 * part + h, half, row] = rad_ref[(2 * h + half) * HROW:(2 * h + half + 1) * HROW, :]

    below, above = lax.rem(y + 3, NY) * 2 + core, lax.rem(y + 1, NY) * 2 + core
    across = lax.rem(y + 2, NY) * 2 + core
    lo, hi = pl.ds(0, GROW), pl.ds(GROW, GROW)
    whole = pl.ds(0, COLS)

    def y_copy(k, src, dst, dev):
        return copy(src, dst, y_s.at[k], y_r.at[k], dev)

    def slot(r, part_):
        return colp.at[r, part_]

    ys = [
        y_copy(0, rad_ref, slot(row, whole), at_y(1)),
        y_copy(1, rad_ref, slot(row, whole), at_y(3)),
        y_copy(2, rad_ref, slot(row, whole), sibling),
        y_copy(3, slot(below, lo), slot(below, lo), at_y(1)),
        y_copy(4, slot(above, hi), slot(above, hi), at_y(3)),
        y_copy(5, slot(below, whole), slot(below, whole), sibling),
        y_copy(6, slot(above, whole), slot(above, whole), sibling),
        y_copy(7, slot(across, lo), slot(across, lo), sibling),
        y_copy(8, slot(across, hi), slot(across, hi), sibling),
    ]
    ys[0].start()
    ys[1].start()
    ys[2].start()
    colp[row, 0:COLS, :] = rad_ref[...]

    def flow_at(f):
        if f == 0:
            return x, 0
        return lax.rem(x + f - 1, NX), 1

    def steps(f, sign):
        return 4 if (f <= 2) == (sign > 0) else 3

    def z_copy(f, sign, s):
        g, half = flow_at(f)
        origin = lax.rem(z + (NZ - s if sign > 0 else s), NZ)
        k = (f * 2 + (0 if sign > 0 else 1)) * 4 + s
        ref = rowp.at[g, half, origin]
        return copy(ref, ref, z_s.at[k], z_r.at[k], at_z(1 if sign > 0 else NZ - 1))

    def z_wait(f, sign, s):
        z_copy(f, sign, s).wait_recv()
        if s + 1 < steps(f, sign):
            z_copy(f, sign, s + 1).start()

    def piece(k):
        d = (k + 1) // 2
        return lax.rem(z + (NZ - d if k % 2 == 1 else d), NZ)

    def xh2(k, sign):
        ref = rowp.at[x, 0, piece(k)]
        n = k if sign > 0 else 8 + k
        return copy(ref, ref, x_s.at[n], x_r.at[n], at_x(1 if sign > 0 else 3))

    def xh2_forward(k):
        sign = 1 if k % 2 == 0 else -1
        ref = rowp.at[lax.rem(x + (3 if sign > 0 else 1), NX), 0, piece(k)]
        return copy(ref, ref, x_s.at[16 + k], x_r.at[16 + k], at_x(1 if sign > 0 else 3))

    def xh2_start(k):
        xh2(k, 1).start()
        xh2(k, -1).start()

    def xh2_wait(k):
        xh2(k, 1).wait_recv()
        xh2(k, -1).wait_recv()
        xh2_forward(k).start()

    def xh1(n):
        ref = rowp.at[lax.rem(x + (3 if n == 2 else 0), NX), 1, z]
        return copy(ref, ref, x_s.at[24 + n], x_r.at[24 + n], at_x(3 if n == 1 else 1))

    def flow_start(f):
        z_copy(f, 1, 0).start()
        z_copy(f, -1, 0).start()

    def sc_wait(half):
        @pl.when(jnp.logical_not(sc_from_self))
        def _():
            sc_copy(0, half).wait_recv()

    sc_wait(0)
    flow_start(0)
    xh2_start(0)
    sc_wait(1)
    flow_start(1)
    xh1(0).start()
    xh1(1).start()

    def spread(i, carry):
        table[i] = jnp.broadcast_to(form_ref[pl.ds(i, 1), :], (16, GRID)).astype(BF)
        return carry

    lax.fori_loop(0, 128, spread, 0, unroll=4)
    ys[0].wait_recv()
    ys[1].wait_recv()
    ys[3].start()
    ys[4].start()
    ys[5].start()
    ys[6].start()
    z_wait(0, 1, 0)
    xh2_start(1)
    z_wait(0, -1, 0)
    xh2_start(2)
    xh1(0).wait_recv()
    xh1(2).start()
    flow_start(4)
    xh1(1).wait_recv()
    flow_start(2)
    xh2_wait(0)
    z_wait(1, 1, 0)
    z_wait(1, -1, 0)
    lax.fori_loop(128, 256, spread, 0, unroll=4)
    z_wait(0, 1, 1)
    xh2_start(3)
    z_wait(0, -1, 1)
    xh2_start(4)
    xh1(2).wait_recv()
    flow_start(3)
    xh2_wait(1)
    xh2_wait(2)
    weighted[...] = (gb_ref[...] * kmat_ref[...].astype(F32)).astype(BF)
    bornp[0:GROW, :] = born_ref[pl.ds(x * GROW, GROW), :]
    z_wait(0, 1, 2)
    xh2_start(5)
    z_wait(0, -1, 2)
    xh2_start(6)
    z_wait(1, 1, 1)
    z_wait(1, -1, 1)
    z_wait(0, 1, 3)
    xh2_start(7)
    ys[3].wait_recv()
    ys[4].wait_recv()
    ys[7].start()
    ys[8].start()
    for f in (4, 2):
        z_wait(f, 1, 0)
        z_wait(f, -1, 0)
    for k in (2, 5, 6, 7, 8):
        ys[k].wait_recv()

    def before_1():
        z_wait(1, 1, 2)
        z_wait(1, -1, 2)
        xh2_wait(3)
        xh2_wait(4)
        z_wait(3, 1, 0)
        z_wait(3, -1, 0)
        z_wait(1, 1, 3)

    def before_2():
        for f in (4, 2):
            z_wait(f, 1, 1)
            z_wait(f, -1, 1)
        for k in (5, 6, 7):
            xh2_wait(k)

    def before_3():
        z_wait(3, 1, 1)
        z_wait(3, -1, 1)

    def before_4():
        for f in (4, 2):
            z_wait(f, 1, 2)
            z_wait(f, -1, 2)
        for k in range(8):
            xh2_forward(k).wait_recv()

    def before_5():
        z_wait(3, 1, 2)
        z_wait(3, -1, 2)
        z_wait(2, 1, 3)

    def before_6():
        z_wait(4, -1, 3)

    def before_7():
        z_wait(3, -1, 3)

    befores = {1: before_1, 2: before_2, 3: before_3, 4: before_4, 5: before_5, 6: before_6, 7: before_7}

    def p_copy(d, half):
        n = (d - 1) * 2 + half
        return copy(psend.at[n], precv.at[n], p_s.at[n], p_r.at[n], at_x(d))

    def v_copy(t, g, half):
        rows = pl.ds(pl.multiple_of(g * GROW + half * HROW, HROW), HROW)
        return pltpu.make_async_copy(vbuf.at[rows], v_out.at[rows], out_s.at[t])

    def batch(t):
        late = jnp.maximum(t - 2, 0)
        third = lax.rem(late, 3)
        d = jnp.where(t < 2, 0, jnp.where(third == 0, 1, jnp.where(third == 1, 3, 2)))
        half = jnp.where((t == 1) | (t >= 5), 1, 0)
        return d, lax.rem(x + d, NX), half

    lanes = lax.broadcasted_iota(jnp.int32, (MOM, 256), 1)

    def build(t, carry):
        for k, fn in befores.items():
            pl.when(t == k)(fn)
        d, g, half = batch(t)
        first = g * GRP + half * HALF
        for w in range(NWIN):
            base = w * WIN * MOM
            start = base // LANE * LANE
            off = base - start
            width = min(256, COLS - start)
            win = jnp.concatenate([colp[c, start:start + 256, :] for c in range(8)], axis=1)
            parts = []
            for i in range(HALF):
                chan = jnp.concatenate(
                    [rowp[g, half, c, i * MOM:(i + 1) * MOM, :] for c in range(8)], axis=1
                ).reshape(3, 16, GRID)
                for j in range(WIN):
                    factor = table[idx_ref[first + i, w * WIN + j]]
                    parts.append((chan * factor[None]).reshape(MOM, GRID))
            scaled = jnp.concatenate(parts, axis=0)
            prod = lax.dot_general(scaled, win, (((1,), (1,)), ((), ())), preferred_element_type=F32)
            for i in range(HALF):
                acc = jnp.zeros((MOM, 256), F32)
                for j in range(WIN):
                    n = i * WIN + j
                    low = off + j * MOM
                    mine = prod[n * MOM:(n + 1) * MOM] * ang_ref[first + i, w * WIN + j]
                    acc = jnp.where((lanes >= low) & (lanes < low + MOM), mine, acc)
                rows = pl.ds(pl.multiple_of((first + i) * MOM, MOM), MOM)
                new = acc.astype(BF)
                if off:
                    new = jnp.where(lanes >= off, new, vbuf[rows, start:start + width])
                vbuf[rows, start:start + width] = new[:, :width]
        rows = pl.ds(pl.multiple_of(g * GROW + half * HROW, HROW), HROW)
        v_copy(t, g, half).start()
        part_sum = jnp.dot(vbuf[rows, :], weighted[...], preferred_element_type=F32)

        @pl.when(d == 0)
        def _():
            pown[half] = part_sum

        @pl.when(d > 0)
        def _():
            n = (d - 1) * 2 + half
            psend[n] = part_sum.astype(BF)
            p_copy(d, half).start()
        return carry

    lax.fori_loop(0, 8, build, 0)

    def tx_copy(d):
        to = lax.rem(x + d, NX)
        return copy(t16.at[pl.ds(to * NZ, NZ)], txrecv.at[d - 1], tx_s.at[d], tx_r.at[d], at_x(d))

    def second(operand):
        turned = operand.T.astype(BF)

        def chunk(q, carry):
            rows = pl.ds(pl.multiple_of(q * 384, 384), 384)
            prod = lax.dot_general(turned, vbuf[rows, :], (((1,), (1,)), ((), ())), preferred_element_type=F32)
            for jj in range(3):
                pbuf[jj] = prod[:, jj * LANE:(jj + 1) * LANE]
            for jj in range(3):
                for c in range(NX * NZ):
                    t32[c, pl.ds(q * 12 + jj * 4, 4), :] = pbuf[jj, 4 * c:4 * c + 4, :]
            return carry

        lax.fori_loop(0, 5, chunk, 0)
        t16[...] = t32[...].astype(BF)
        for d in (2, 1, 3):
            tx_copy(d).start()

    @pl.when(jnp.logical_not(in_slab))
    def _():
        second(weighted[...].astype(F32))

    for n in range(6):
        p_copy(n // 2 + 1, n % 2).wait_recv()
    for half in range(2):
        total = pown[half]
        for d in range(3):
            total = total + precv[d * 2 + half].astype(F32)
        ssum[half * HROW:(half + 1) * HROW, :] = total
        zsend[half * HROW:(half + 1) * HROW, :] = total.astype(BF)

    def shard(q):
        return pl.ds(pl.multiple_of(q * SH, SH), SH)

    def r_copy(d):
        return copy(zsend.at[shard(lax.rem(z + d, NZ))], zrecv.at[d - 1], r_s.at[d], r_r.at[d], at_z(d))

    for d in range(1, NZ):
        r_copy(d).start()
    for d in range(1, NZ):
        r_copy(d).wait_recv()
    total = bornp[shard(z), :] + ssum[shard(z), :]
    for d in range(NZ - 1):
        total = total + zrecv[d].astype(F32)
    fresh = total.astype(BF)
    fi[x, shard(z), :] = fresh
    g_part = lax.rem(x, 2)

    def u_copy(k):
        src = fi.at[x, shard(z)]
        return copy(src, upd.at[g_part, shard(z)], u_s.at[k], u_r.at[g_part * NZ + z], (lax.rem(row + k, NROW), use_col))

    for k in range(NROW):
        if k == 0:
            @pl.when(use_self)
            def _():
                upd[g_part, shard(z), :] = fresh

            @pl.when(jnp.logical_not(use_self))
            def _():
                u_copy(0).start()
        else:
            u_copy(k).start()

    def fz_copy(d):
        ref = fi.at[x, shard(z)]
        return copy(ref, ref, fz_s.at[d], fz_r.at[d], at_z(d))

    for d in range(1, NZ):
        fz_copy(d).start()

    @pl.when(in_slab)
    def _():
        for k in range(2 * NZ):
            ref = upd.at[k // NZ, pl.ds(k % NZ * SH, SH)]

            @pl.when(jnp.logical_not(source_self & (g_part * NZ + z == k)))
            def _():
                copy(ref, ref, u_s.at[0], u_r.at[k], sibling).wait_recv()
        fresh_rows = jnp.concatenate([upd[0, 0:GROW, :], upd[1, 0:GROW, :]], axis=0)
        second((gb_ref[...] * fresh_rows.astype(F32)).astype(BF).astype(F32))

    for d in range(1, NZ):
        ref = fi.at[x, shard(lax.rem(z + NZ - d, NZ))]
        copy(ref, ref, fz_s.at[d], fz_r.at[d], at_z(d)).wait_recv()

    def fx_copy(d, g):
        ref = fi.at[g, pl.ds(0, GROW)]
        return copy(ref, ref, fx_s.at[d], fx_r.at[d], at_x(d))

    for d in (2, 1, 3):
        fx_copy(d, x).start()

    for d in range(1, NX):
        tx_copy(d).wait_recv()
    total = t32[pl.ds(x * NZ, NZ)]
    for d in range(NX - 1):
        total = total + txrecv[d].astype(F32)
    tz32[...] = total
    tzsend[...] = total.astype(BF)

    def tz_copy(d):
        return copy(tzsend.at[lax.rem(z + d, NZ)], tzrecv.at[d - 1], tz_s.at[d], tz_r.at[d], at_z(d))

    for d in range(1, NZ):
        tz_copy(d).start()
    for d in range(1, NX):
        fx_copy(d, lax.rem(x + NX - d, NX)).wait_recv()

    def f_out(g):
        return pltpu.make_async_copy(fi.at[g, pl.ds(0, GROW)], first_out.at[pl.ds(g * GROW, GROW)], out_s.at[8 + g])

    for g in range(NX):
        f_out(g).start()
    for d in range(1, NZ):
        tz_copy(d).wait_recv()
    total = tz32[z]
    for d in range(NZ - 1):
        total = total + tzrecv[d].astype(F32)
    share_out[...] = total

    for g in range(NX):
        f_out(g).wait()

    def v_wait(t, carry):
        _, g, half = batch(t)
        v_copy(t, g, half).wait()
        return carry

    lax.fori_loop(0, 8, v_wait, 0)
    for h in range(2):
        @pl.when(in_slab & jnp.logical_not(scatter_self(h)))
        def _():
            for half in range(2):
                sc_copy(h, half).wait_send()
    for c in ys:
        c.wait_send()
    for f in range(5):
        for sign in (1, -1):
            for s in range(steps(f, sign)):
                z_copy(f, sign, s).wait_send()
    for k in range(8):
        xh2(k, 1).wait_send()
        xh2(k, -1).wait_send()
        xh2_forward(k).wait_send()
    for n in range(3):
        xh1(n).wait_send()
    for n in range(6):
        p_copy(n // 2 + 1, n % 2).wait_send()
    for d in range(1, NZ):
        r_copy(d).wait_send()
        fz_copy(d).wait_send()
        tz_copy(d).wait_send()
    for d in range(1, NX):
        fx_copy(d, x).wait_send()
        tx_copy(d).wait_send()

    @pl.when(jnp.logical_not(use_self))
    def _():
        u_copy(0).wait_send()

    for k in range(1, NROW):
        u_copy(k).wait_send()


def body(radial, form_factors, coupling, quantum, green_diag, kmatrix, born_term):
    row_count, col_count = coupling.shape
    row_index, col_index = lax.axis_index("row"), lax.axis_index("col")
    rq = lax.dynamic_slice_in_dim(quantum, row_index * row_count, row_count, 0)
    cq = lax.dynamic_slice_in_dim(quantum, col_index * col_count, col_count, 0)
    table_index = coupling * (NTARG * NTARG) + rq[:, 2:3] * NTARG + cq[:, 2][None, :]
    parity = (rq[:, 0:1] + cq[:, 0][None, :]) % 2
    spread_m = jnp.abs(rq[:, 1:2] - cq[:, 1][None, :])
    angular = (1.0 - 2.0 * parity.astype(F32)) / (1.0 + spread_m.astype(F32))
    green = jnp.broadcast_to(green_diag.reshape(COLS, 1), (COLS, LANE))
    vm = pl.BlockSpec(memory_space=pltpu.VMEM)
    sm = pl.BlockSpec(memory_space=pltpu.SMEM)
    hb = pl.BlockSpec(memory_space=pl.ANY)
    dma = pltpu.SemaphoreType.DMA
    v_block, first, share = pl.pallas_call(
        kernel,
        out_shape=(
            jax.ShapeDtypeStruct((ROWS, COLS), BF),
            jax.ShapeDtypeStruct((ROWS, LANE), BF),
            jax.ShapeDtypeStruct((SH, LANE), F32),
        ),
        in_specs=[sm, sm, vm, vm, vm, vm, vm],
        out_specs=(hb, hb, vm),
        scratch_shapes=[
            pltpu.VMEM((256, 16, GRID), BF),
            pltpu.VMEM((NROW, 1024, LANE), BF),
            pltpu.VMEM((NX, 2, NROW, HROW, LANE), BF),
            pltpu.VMEM((ROWS, COLS), BF),
            pltpu.VMEM((COLS, LANE), BF),
            pltpu.VMEM((2, HROW, LANE), F32),
            pltpu.VMEM((6, HROW, LANE), BF),
            pltpu.VMEM((6, HROW, LANE), BF),
            pltpu.VMEM((NZ * SH, LANE), F32),
            pltpu.VMEM((NZ * SH, LANE), BF),
            pltpu.VMEM((NZ - 1, SH, LANE), BF),
            pltpu.VMEM((NZ * SH, LANE), F32),
            pltpu.VMEM((NX, NZ * SH, LANE), BF),
            pltpu.VMEM((2, NZ * SH, LANE), BF),
            pltpu.VMEM((NX * NZ, SH, LANE), F32),
            pltpu.VMEM((NX * NZ, SH, LANE), BF),
            pltpu.VMEM((3, LANE, LANE), F32),
            pltpu.VMEM((NX - 1, NZ, SH, LANE), BF),
            pltpu.VMEM((NZ, SH, LANE), F32),
            pltpu.VMEM((NZ, SH, LANE), BF),
            pltpu.VMEM((NZ - 1, SH, LANE), BF),
            dma((4,)), dma((2,)), dma((9,)), dma((9,)), dma((40,)), dma((40,)), dma((27,)), dma((27,)),
            dma((6,)), dma((6,)), dma((8,)), dma((8,)), dma((8,)), dma((16,)),
            dma((8,)), dma((8,)), dma((4,)), dma((4,)), dma((4,)), dma((4,)), dma((8,)), dma((8,)), dma((12,)),
        ],
        compiler_params=pltpu.CompilerParams(collective_id=0, has_side_effects=True, vmem_limit_bytes=56 << 20),
        name="sweeps",
    )(table_index, angular, radial.reshape(COLS, LANE), form_factors, green, kmatrix, born_term)
    born_share = lax.dynamic_slice_in_dim(born_term, col_index * 4, 4, 1)
    col_share = share[:60].reshape(15, 4, LANE).transpose(0, 2, 1).reshape(ROWS, 4)
    return v_block, first, born_share + col_share


def solution(mesh):
    placed = (
        P("col", None, "row"),
        P(),
        P("row", "col"),
        P(),
        P("col", None),
        P("col", None),
        P("row", None),
    )
    return jax.shard_map(
        body,
        mesh=mesh,
        in_specs=placed,
        out_specs=(P("row", "col"), P("row", None), P("row", "col")),
        check_vma=False,
    )
```

```python
import functools

import jax
import jax.numpy as jnp
from jax import lax
from jax.experimental import pallas as pl
from jax.experimental.pallas import tpu as pltpu
from jax.sharding import PartitionSpec as P

NTARG = 4
MESH = pl.DeviceIdType.MESH
BF, F32 = jnp.bfloat16, jnp.float32

NX, NZ, NY = 4, 8, 4
NROW = 8
MOM = 48
GRID = 1024
LANE = 128
NB = 20
HALF = 5
HROW = HALF * MOM
COLS = NB * MOM
MID = COLS // 2
ROWS = 2 * COLS
SH = 64
PAD = 4 * SH
WIN = 4
NWIN = NB // WIN


def kernel(code_ref, rad_ref, form_hbm, green_ref, kmat_ref, born_hbm,
           v_out, first_out, share_out,
           sign, table, form_ref, colp, rowp, mid, vbuf, vturn, gb_ref, weighted, pown, psend, precv, ssum, zsend, zrecv,
           born_ref, bornp, bturn, fi, upd, t32, t16, pbuf, txrecv, tz32, tzsend, tzrecv,
           s1_s, s1_r, s2_s, s2_r, y_s, y_r, z_s, z_r, x_s, x_r, p_s, p_r, r_s, r_r, u_s, u_r, b_s, b_r, f_s,
           fz_s, fz_r, fx_s, fx_r, tx_s, tx_r, tz_s, tz_r, in_s, out_s):
    row = lax.axis_index("row")
    col = lax.axis_index("col")
    x, z = col // NZ, col % NZ
    y, core = row // 2, row % 2

    def at_x(d):
        return (row, lax.rem(x + d, NX) * NZ + z)

    def at_z(d):
        return (row, x * NZ + lax.rem(z + d, NZ))

    def at_y(d):
        return (lax.rem(y + d, NY) * 2 + core, col)

    sibling = (y * 2 + 1 - core, col)
    in_slab = col < 2 * NROW

    def shift(r, xs):
        k = lax.rem(r // 2 + 2 * xs, 4)
        return jnp.where(lax.rem(r, 2) == 0, k, jnp.where(k == 0, 4, 8 - k))

    def s2_to(xs):
        return 4 * xs + z // 2, lax.rem(z + shift(row, xs), NZ)

    def s2_self(xs):
        to_row, to_z = s2_to(xs)
        return (to_row == row) & (to_z == z)

    def s2_from(half):
        xs, zs = row // 4, lax.rem(2 * row + half, NZ)
        s = lax.rem(z - zs + NZ, NZ)
        k = lax.rem(jnp.minimum(s, NZ - s) + 2 * xs, 4)
        return 2 * k + (s >= 4).astype(jnp.int32), zs

    def s2_from_self(half):
        r, zs = s2_from(half)
        return (r == row) & (zs == z)

    part = col % 2
    use_col = 2 * row + z // 4
    use_self = use_col == col
    home = in_slab & (col // 2 == row)
    home_y, home_core = (col // 2) // 2, (col // 2) % 2

    def copy(src, dst, ss, rs, dev):
        return pltpu.make_async_remote_copy(src_ref=src, dst_ref=dst, send_sem=ss, recv_sem=rs,
                                            device_id=dev, device_id_type=MESH)

    bar = pltpu.get_barrier_semaphore()

    def greet(dev):
        pl.semaphore_signal(bar, inc=1, device_id=dev, device_id_type=MESH)

    for d in range(1, NZ):
        greet(at_z(d))
    for d in range(1, NX):
        greet(at_x(d))
    for d in range(1, NY):
        greet(at_y(d))
    greet(sibling)
    for half in range(2):
        @pl.when(jnp.logical_not(s2_from_self(half)))
        def _():
            r, zs = s2_from(half)
            greet((r, x * NZ + zs))

    @pl.when(home)
    def _():
        def hello(k, carry):
            xx, zz = k // 4, 4 * part + lax.rem(k, 4)

            @pl.when(xx * NZ + zz != col)
            def _():
                greet((row, xx * NZ + zz))
            return carry

        lax.fori_loop(0, 16, hello, 0)

    loads = [pltpu.make_async_copy(form_hbm, form_ref, in_s.at[0]), pltpu.make_async_copy(born_hbm, born_ref, in_s.at[1])]
    for c in loads:
        c.start()
    for k in range(8):
        sign[k] = jnp.float32((1.0 - 2.0 * (k // 4)) / (1.0 + k % 4))
    colp[:, COLS:, :] = jnp.zeros((NROW, 1024 - COLS, LANE), BF)
    for half in range(2):
        edge = slice(half * PAD + HROW, (half + 1) * PAD)
        zsend[edge, :] = jnp.zeros((PAD - HROW, LANE), BF)
        ssum[edge, :] = jnp.zeros((PAD - HROW, LANE), F32)
        bornp[edge, :] = jnp.zeros((PAD - HROW, LANE), F32)
    t32[:, 60:, :] = jnp.zeros((NX * NZ, 4, LANE), F32)

    n_wait = 7 + 3 + 3 + 1 + 1 - use_self.astype(jnp.int32) + 2
    for xs in range(2):
        n_wait = n_wait - s2_self(xs).astype(jnp.int32)
    pl.semaphore_wait(bar, n_wait)

    def s1_copy(d):
        g = lax.rem(x + d, NX)
        src = rad_ref.at[pl.ds(pl.multiple_of(g * HROW, HROW), HROW)]
        return copy(src, mid.at[x], s1_s.at[d], s1_r.at[x], at_x(d))

    @pl.when(in_slab)
    def _():
        for d in (2, 1, 3):
            s1_copy(d).start()
        mid[x] = rad_ref[pl.ds(pl.multiple_of(x * HROW, HROW), HROW), :]

    below, above = lax.rem(y + 3, NY) * 2 + core, lax.rem(y + 1, NY) * 2 + core
    across = lax.rem(y + 2, NY) * 2 + core
    lo, hi = pl.ds(0, MID), pl.ds(MID, MID)

    def y_copy(k, src, dst, dev):
        return copy(src, dst, y_s.at[k], y_r.at[k], dev)

    def y_part(k, r, part_, dev):
        return y_copy(k, colp.at[r, part_], colp.at[r, part_], dev)

    ys = [
        y_copy(0, rad_ref.at[lo], colp.at[row, lo], at_y(1)),
        y_copy(1, rad_ref.at[hi], colp.at[row, hi], at_y(3)),
        y_copy(2, rad_ref.at[hi], colp.at[row, hi], at_y(1)),
        y_copy(3, rad_ref.at[lo], colp.at[row, lo], at_y(3)),
        y_copy(4, rad_ref, colp.at[row, pl.ds(0, COLS)], sibling),
        y_part(5, below, lo, at_y(1)),
        y_part(6, above, hi, at_y(3)),
        y_part(7, below, lo, sibling),
        y_part(8, above, hi, sibling),
        y_part(9, below, hi, sibling),
        y_part(10, above, lo, sibling),
        y_part(11, across, lo, sibling),
        y_part(12, across, hi, sibling),
    ]
    for k in range(5):
        ys[k].start()
    colp[row, 0:COLS, :] = rad_ref[...]

    def s2_copy(xs):
        to_row, to_z = s2_to(xs)
        half = lax.rem(z, 2)
        return copy(mid.at[xs], rowp.at[x, half, to_z], s2_s.at[xs], s2_r.at[half], (to_row, x * NZ + to_z))

    for xs in range(2):
        @pl.when(x != xs)
        def _():
            copy(mid.at[xs], mid.at[xs], s1_s.at[0], s1_r.at[xs], sibling).wait_recv()

        @pl.when(s2_self(xs))
        def _():
            rowp[x, lax.rem(z, 2), z] = mid[xs]

        @pl.when(jnp.logical_not(s2_self(xs)))
        def _():
            s2_copy(xs).start()

    def flow_at(f):
        if f == 0:
            return x, 0
        return lax.rem(x + f - 1, NX), 1

    def steps(f, sign):
        return 4 if (f <= 2) == (sign > 0) else 3

    def z_copy(f, sign, s):
        g, half = flow_at(f)
        origin = lax.rem(z + (NZ - s if sign > 0 else s), NZ)
        k = (f * 2 + (0 if sign > 0 else 1)) * 4 + s
        ref = rowp.at[g, half, origin]
        return copy(ref, ref, z_s.at[k], z_r.at[k], at_z(1 if sign > 0 else NZ - 1))

    def z_wait(f, sign, s):
        z_copy(f, sign, s).wait_recv()
        if s + 1 < steps(f, sign):
            z_copy(f, sign, s + 1).start()

    def piece(k):
        d = (k + 1) // 2
        return lax.rem(z + (NZ - d if k % 2 == 1 else d), NZ)

    def xh2(k, sign):
        ref = rowp.at[x, 0, piece(k)]
        n = k if sign > 0 else 8 + k
        return copy(ref, ref, x_s.at[n], x_r.at[n], at_x(1 if sign > 0 else 3))

    def xh2_forward(k):
        sign = 1 if k % 2 == 0 else -1
        ref = rowp.at[lax.rem(x + (3 if sign > 0 else 1), NX), 0, piece(k)]
        return copy(ref, ref, x_s.at[16 + k], x_r.at[16 + k], at_x(1 if sign > 0 else 3))

    def xh2_start(k):
        xh2(k, 1).start()
        xh2(k, -1).start()

    def xh2_wait(k):
        xh2(k, 1).wait_recv()
        xh2(k, -1).wait_recv()
        xh2_forward(k).start()

    def xh1(n):
        ref = rowp.at[lax.rem(x + (3 if n == 2 else 0), NX), 1, z]
        return copy(ref, ref, x_s.at[24 + n], x_r.at[24 + n], at_x(3 if n == 1 else 1))

    def flow_start(f):
        z_copy(f, 1, 0).start()
        z_copy(f, -1, 0).start()

    def sc_wait(half):
        @pl.when(jnp.logical_not(s2_from_self(half)))
        def _():
            ref = rowp.at[x, half, z]
            copy(ref, ref, s2_s.at[0], s2_r.at[half], sibling).wait_recv()

    sc_wait(0)
    flow_start(0)
    xh2_start(0)
    sc_wait(1)
    flow_start(1)
    xh1(0).start()
    xh1(1).start()

    def spread(i, carry):
        table[i] = jnp.broadcast_to(form_ref[pl.ds(i, 1), :], (16, GRID)).astype(BF)
        return carry

    def y_on(k, *then):
        ys[k].wait_recv()
        for n in then:
            ys[n].start()

    for c in loads:
        c.wait()
    lax.fori_loop(0, 64, spread, 0, unroll=4)
    y_on(0, 5, 7)
    y_on(1, 6, 8)
    y_on(2, 9)
    y_on(3, 10)
    z_wait(0, 1, 0)
    xh2_start(1)
    z_wait(0, -1, 0)
    xh2_start(2)
    xh1(0).wait_recv()
    xh1(2).start()
    flow_start(4)
    xh1(1).wait_recv()
    flow_start(2)
    xh2_wait(0)
    z_wait(1, 1, 0)
    z_wait(1, -1, 0)
    lax.fori_loop(64, 160, spread, 0, unroll=4)
    z_wait(0, 1, 1)
    xh2_start(3)
    z_wait(0, -1, 1)
    xh2_start(4)
    xh1(2).wait_recv()
    flow_start(3)
    xh2_wait(1)
    xh2_wait(2)
    lax.fori_loop(160, 256, spread, 0, unroll=4)
    for b in range(NB):
        gb_ref[b * MOM:(b + 1) * MOM, :] = jnp.broadcast_to(green_ref[b:b + 1, :], (LANE, MOM)).T
    weighted[...] = (gb_ref[...] * kmat_ref[...].astype(F32)).astype(BF)
    for half in range(2):
        bornp[half * PAD:half * PAD + HROW, :] = born_ref[pl.ds(pl.multiple_of(half * COLS + x * HROW, HROW), HROW), :]
    z_wait(0, 1, 2)
    xh2_start(5)
    z_wait(0, -1, 2)
    xh2_start(6)
    z_wait(1, 1, 1)
    z_wait(1, -1, 1)
    z_wait(0, 1, 3)
    xh2_start(7)
    y_on(5, 11)
    y_on(6, 12)
    for f in (4, 2):
        z_wait(f, 1, 0)
        z_wait(f, -1, 0)
    for k in (4, 7, 8, 9, 10, 11, 12):
        ys[k].wait_recv()

    def before_1():
        z_wait(1, 1, 2)
        z_wait(1, -1, 2)
        xh2_wait(3)
        xh2_wait(4)
        z_wait(3, 1, 0)
        z_wait(3, -1, 0)
        z_wait(1, 1, 3)

    def before_2():
        for f in (4, 2):
            z_wait(f, 1, 1)
            z_wait(f, -1, 1)
        for k in (5, 6, 7):
            xh2_wait(k)

    def before_3():
        z_wait(3, 1, 1)
        z_wait(3, -1, 1)

    def before_4():
        for f in (4, 2):
            z_wait(f, 1, 2)
            z_wait(f, -1, 2)
        for k in range(8):
            xh2_forward(k).wait_recv()

    def before_5():
        z_wait(3, 1, 2)
        z_wait(3, -1, 2)
        z_wait(2, 1, 3)

    def before_6():
        z_wait(4, -1, 3)

    def before_7():
        z_wait(3, -1, 3)

    befores = {1: before_1, 2: before_2, 3: before_3, 4: before_4, 5: before_5, 6: before_6, 7: before_7}

    def p_copy(d, half):
        n = (d - 1) * 2 + half
        return copy(psend.at[n], precv.at[n], p_s.at[n], p_r.at[n], at_x(d))

    def batch(t):
        late = jnp.maximum(t - 2, 0)
        third = lax.rem(late, 3)
        d = jnp.where(t < 2, 0, jnp.where(third == 0, 1, jnp.where(third == 1, 3, 2)))
        half = jnp.where((t == 1) | (t >= 5), 1, 0)
        return d, lax.rem(x + d, NX), half

    lanes = lax.broadcasted_iota(jnp.int32, (MOM, 256), 1)

    def build(t, carry):
        for k, fn in befores.items():
            pl.when(t == k)(fn)
        d, g, half = batch(t)
        first = half * NB + g * HALF
        zs = lax.rem(2 * row + half, NZ)
        slots = [lax.rem(zs + shift(jnp.int32(r), row // 4), NZ) for r in range(NROW)]
        for w in range(NWIN):
            base = w * WIN * MOM
            start = base // LANE * LANE
            off = base - start
            width = min(256, COLS - start)
            win = jnp.concatenate([colp[c, start:start + 256, :] for c in range(8)], axis=1)
            parts = []
            for i in range(HALF):
                chan = jnp.concatenate(
                    [rowp[g, half, slots[c], i * MOM:(i + 1) * MOM, :] for c in range(NROW)], axis=1
                ).reshape(3, 16, GRID)
                for j in range(WIN):
                    factor = table[code_ref[w * WIN + j, first + i] & 255]
                    parts.append((chan * factor[None]).reshape(MOM, GRID))
            scaled = jnp.concatenate(parts, axis=0)
            prod = lax.dot_general(scaled, win, (((1,), (1,)), ((), ())), preferred_element_type=F32)
            for i in range(HALF):
                acc = jnp.zeros((MOM, 256), F32)
                for j in range(WIN):
                    n = i * WIN + j
                    low = off + j * MOM
                    mine = prod[n * MOM:(n + 1) * MOM] * sign[code_ref[w * WIN + j, first + i] >> 8]
                    acc = jnp.where((lanes >= low) & (lanes < low + MOM), mine, acc)
                rows = pl.ds(pl.multiple_of((first + i) * MOM, MOM), MOM)
                new = acc.astype(BF)
                if off:
                    new = jnp.where(lanes >= off, new, vbuf[rows, start:start + width])
                vbuf[rows, start:start + width] = new[:, :width]
        rows = pl.ds(pl.multiple_of(first * MOM, HROW), HROW)
        part_sum = jnp.dot(vbuf[rows, :], weighted[...], preferred_element_type=F32)

        @pl.when(d == 0)
        def _():
            pown[half] = part_sum

        @pl.when(d > 0)
        def _():
            n = (d - 1) * 2 + half
            psend[n] = part_sum.astype(BF)
            p_copy(d, half).start()
        return carry

    lax.fori_loop(0, 8, build, 0)

    def tx_copy(d):
        to = lax.rem(x + d, NX)
        return copy(t16.at[pl.ds(to * NZ, NZ)], txrecv.at[d - 1], tx_s.at[d], tx_r.at[d], at_x(d))

    def second(operand):
        turned = operand.T.astype(BF)

        def chunk(q, carry):
            rows = pl.ds(pl.multiple_of(q * 384, 384), 384)
            prod = lax.dot_general(turned, vbuf[rows, :], (((1,), (1,)), ((), ())), preferred_element_type=F32)
            for jj in range(3):
                pbuf[jj] = prod[:, jj * LANE:(jj + 1) * LANE]
            for jj in range(3):
                for c in range(NX * NZ):
                    t32[c, pl.ds(q * 12 + jj * 4, 4), :] = pbuf[jj, 4 * c:4 * c + 4, :]
            return carry

        lax.fori_loop(0, 5, chunk, 0)
        t16[...] = t32[...].astype(BF)
        for d in (2, 1, 3):
            tx_copy(d).start()

    def turn(m, carry):
        at = pl.ds(pl.multiple_of(m * LANE, LANE), LANE)
        vturn[:, at] = vbuf[at, :].T
        return carry

    @pl.when(jnp.logical_not(in_slab))
    def _():
        second(weighted[...].astype(F32))

    for n in range(6):
        p_copy(n // 2 + 1, n % 2).wait_recv()
    for half in range(2):
        total = pown[half]
        for d in range(3):
            total = total + precv[d * 2 + half].astype(F32)
        ssum[half * PAD:half * PAD + HROW, :] = total
        zsend[half * PAD:half * PAD + HROW, :] = total.astype(BF)

    def shard(q):
        return pl.ds(pl.multiple_of(q * SH, SH), SH)

    def r_copy(d):
        return copy(zsend.at[shard(lax.rem(z + d, NZ))], zrecv.at[d - 1], r_s.at[d], r_r.at[d], at_z(d))

    for d in range(1, NZ):
        r_copy(d).start()
    lax.fori_loop(0, 4, turn, 0)
    for d in range(1, NZ):
        r_copy(d).wait_recv()
    total = bornp[shard(z), :] + ssum[shard(z), :]
    for d in range(NZ - 1):
        total = total + zrecv[d].astype(F32)
    fresh = total.astype(BF)
    fi[x, shard(z), :] = fresh
    def u_copy():
        return copy(fi.at[x, shard(z)], upd.at[x, shard(lax.rem(z, 4))], u_s.at[0], u_r.at[x * 4 + lax.rem(z, 4)],
                    (row, use_col))

    @pl.when(use_self)
    def _():
        upd[x, shard(lax.rem(z, 4)), :] = fresh

    @pl.when(jnp.logical_not(use_self))
    def _():
        u_copy().start()

    def fz_copy(d):
        ref = fi.at[x, shard(z)]
        return copy(ref, ref, fz_s.at[d], fz_r.at[d], at_z(d))

    for d in range(1, NZ):
        fz_copy(d).start()

    def b_copy(d, g):
        ref = upd.at[g, pl.ds(0, HROW)]
        return copy(ref, ref, b_s.at[d * 4 + g], b_r.at[g], sibling if d == 0 else at_y(d))

    def f_copy(g):
        ref = upd.at[g, pl.ds(0, HROW)]
        return copy(ref, ref, f_s.at[g], b_r.at[g], sibling)

    @pl.when(home)
    def _():
        for g in range(NX):
            for q in range(4):
                @pl.when(g * NZ + 4 * part + q != col)
                def _():
                    ref = upd.at[g, pl.ds(q * SH, SH)]
                    copy(ref, ref, u_s.at[0], u_r.at[g * 4 + q], sibling).wait_recv()
            for d in (2, 1, 3, 0):
                b_copy(d, g).start()

    lax.fori_loop(4, 8, turn, 0)
    for d in range(1, NZ):
        ref = fi.at[x, shard(lax.rem(z + NZ - d, NZ))]
        copy(ref, ref, fz_s.at[d], fz_r.at[d], at_z(d)).wait_recv()

    def fx_copy(d, g):
        return copy(fi.at[g], fi.at[g], fx_s.at[d], fx_r.at[d], at_x(d))

    for d in (2, 1, 3):
        fx_copy(d, x).start()

    @pl.when(in_slab)
    def _():
        @pl.when(jnp.logical_not(home))
        def _():
            for g in range(NX):
                f_copy(g).wait_recv()

                @pl.when((core == home_core) & (y != home_y))
                def _():
                    f_copy(g).start()
        fresh_rows = jnp.concatenate([upd[g, 0:HROW, :] for g in range(NX)], axis=0)
        second((gb_ref[...] * fresh_rows.astype(F32)).astype(BF).astype(F32))

    lax.fori_loop(8, 15, turn, 0)

    def v_copy():
        return pltpu.make_async_copy(vturn, v_out, out_s.at[8])

    v_copy().start()
    for j in range(15):
        bturn[j] = born_ref[j * LANE:(j + 1) * LANE, :].T

    for d in range(1, NX):
        tx_copy(d).wait_recv()
    total = t32[pl.ds(x * NZ, NZ)]
    for d in range(NX - 1):
        total = total + txrecv[d].astype(F32)
    tz32[...] = total
    tzsend[...] = total.astype(BF)

    def tz_copy(d):
        return copy(tzsend.at[lax.rem(z + d, NZ)], tzrecv.at[d - 1], tz_s.at[d], tz_r.at[d], at_z(d))

    for d in range(1, NZ):
        tz_copy(d).start()
    for d in range(1, NX):
        fx_copy(d, lax.rem(x + NX - d, NX)).wait_recv()

    def f_out(g, half):
        return pltpu.make_async_copy(fi.at[g, pl.ds(half * PAD, HROW)],
                                     first_out.at[pl.ds(half * COLS + g * HROW, HROW)], out_s.at[2 * g + half])

    for g in range(NX):
        for half in range(2):
            f_out(g, half).start()
    for d in range(1, NZ):
        tz_copy(d).wait_recv()
    total = tz32[z]
    for d in range(NZ - 1):
        total = total + tzrecv[d].astype(F32)
    tz32[z] = total
    for j in range(15):
        share_out[:, j * LANE:(j + 1) * LANE] = tz32[z, 4 * j:4 * j + 4, :] + bturn[j, pl.ds(4 * col, 4), :]

    for g in range(NX):
        for half in range(2):
            f_out(g, half).wait()
    v_copy().wait()

    @pl.when(in_slab)
    def _():
        for d in range(1, NX):
            s1_copy(d).wait_send()

    for xs in range(2):
        @pl.when(jnp.logical_not(s2_self(xs)))
        def _():
            s2_copy(xs).wait_send()
    for c in ys:
        c.wait_send()
    for f in range(5):
        for sign in (1, -1):
            for s in range(steps(f, sign)):
                z_copy(f, sign, s).wait_send()
    for k in range(8):
        xh2(k, 1).wait_send()
        xh2(k, -1).wait_send()
        xh2_forward(k).wait_send()
    for n in range(3):
        xh1(n).wait_send()
    for n in range(6):
        p_copy(n // 2 + 1, n % 2).wait_send()
    for d in range(1, NZ):
        r_copy(d).wait_send()
        fz_copy(d).wait_send()
        tz_copy(d).wait_send()
    for d in range(1, NX):
        fx_copy(d, x).wait_send()
        tx_copy(d).wait_send()

    @pl.when(jnp.logical_not(use_self))
    def _():
        u_copy().wait_send()

    @pl.when(home)
    def _():
        for g in range(NX):
            for d in range(4):
                b_copy(d, g).wait_send()

    @pl.when(in_slab & jnp.logical_not(home) & (core == home_core) & (y != home_y))
    def _():
        for g in range(NX):
            f_copy(g).wait_send()


def body(radial, form_factors, coupling, quantum, green_diag, kmatrix, born_term):
    row_count, col_count = coupling.shape
    row_index, col_index = lax.axis_index("row"), lax.axis_index("col")
    rq = lax.dynamic_slice_in_dim(quantum, row_index * row_count, row_count, 0)
    cq = lax.dynamic_slice_in_dim(quantum, col_index * col_count, col_count, 0)
    table_index = coupling * (NTARG * NTARG) + rq[:, 2:3] * NTARG + cq[:, 2][None, :]
    parity = (rq[:, 0:1] + cq[:, 0][None, :]) % 2
    spread_m = jnp.abs(rq[:, 1:2] - cq[:, 1][None, :])
    code = (table_index + 256 * (4 * parity + spread_m)).T
    vm = pl.BlockSpec(memory_space=pltpu.VMEM)
    sm = pl.BlockSpec(memory_space=pltpu.SMEM)
    hb = pl.BlockSpec(memory_space=pl.ANY)
    dma = pltpu.SemaphoreType.DMA
    v_block, first, share = pl.pallas_call(
        kernel,
        out_shape=(
            jax.ShapeDtypeStruct((COLS, ROWS), BF),
            jax.ShapeDtypeStruct((ROWS, LANE), BF),
            jax.ShapeDtypeStruct((4, ROWS), F32),
        ),
        in_specs=[sm, vm, hb, vm, vm, hb],
        out_specs=(hb, hb, vm),
        scratch_shapes=[
            pltpu.SMEM((8,), F32),
            pltpu.VMEM((256, 16, GRID), BF),
            pltpu.VMEM((256, GRID), F32),
            pltpu.VMEM((NROW, 1024, LANE), BF),
            pltpu.VMEM((NX, 2, NROW, HROW, LANE), BF),
            pltpu.VMEM((2, HROW, LANE), BF),
            pltpu.VMEM((ROWS, COLS), BF),
            pltpu.VMEM((COLS, ROWS), BF),
            pltpu.VMEM((COLS, LANE), F32),
            pltpu.VMEM((COLS, LANE), BF),
            pltpu.VMEM((2, HROW, LANE), F32),
            pltpu.VMEM((6, HROW, LANE), BF),
            pltpu.VMEM((6, HROW, LANE), BF),
            pltpu.VMEM((2 * PAD, LANE), F32),
            pltpu.VMEM((2 * PAD, LANE), BF),
            pltpu.VMEM((NZ - 1, SH, LANE), BF),
            pltpu.VMEM((ROWS, LANE), F32),
            pltpu.VMEM((2 * PAD, LANE), F32),
            pltpu.VMEM((15, LANE, LANE), F32),
            pltpu.VMEM((NX, 2 * PAD, LANE), BF),
            pltpu.VMEM((NX, PAD, LANE), BF),
            pltpu.VMEM((NX * NZ, SH, LANE), F32),
            pltpu.VMEM((NX * NZ, SH, LANE), BF),
            pltpu.VMEM((3, LANE, LANE), F32),
            pltpu.VMEM((NX - 1, NZ, SH, LANE), BF),
            pltpu.VMEM((NZ, SH, LANE), F32),
            pltpu.VMEM((NZ, SH, LANE), BF),
            pltpu.VMEM((NZ - 1, SH, LANE), BF),
            dma((4,)), dma((2,)), dma((2,)), dma((2,)), dma((13,)), dma((13,)), dma((40,)), dma((40,)), dma((27,)), dma((27,)),
            dma((6,)), dma((6,)), dma((8,)), dma((8,)), dma((1,)), dma((16,)), dma((16,)), dma((4,)), dma((4,)),
            dma((8,)), dma((8,)), dma((4,)), dma((4,)), dma((4,)), dma((4,)), dma((8,)), dma((8,)), dma((2,)), dma((9,)),
        ],
        compiler_params=pltpu.CompilerParams(collective_id=0, has_side_effects=True, vmem_limit_bytes=58 << 20),
        name="sweeps",
    )(code, radial.reshape(COLS, LANE), form_factors, green_diag, kmatrix, born_term)
    return v_block.T, first, share.T


def solution(mesh):
    placed = (
        P("col", None, "row"),
        P(),
        P("row", "col"),
        P(),
        P("col", None),
        P("col", None),
        P("row", None),
    )
    return jax.shard_map(
        body,
        mesh=mesh,
        in_specs=placed,
        out_specs=(P("row", "col"), P("row", None), P("row", "col")),
        check_vma=False,
    )
```

```python
import functools

import jax
import jax.numpy as jnp
from jax import lax
from jax.experimental import pallas as pl
from jax.experimental.pallas import tpu as pltpu
from jax.sharding import PartitionSpec as P

NTARG = 4
MESH = pl.DeviceIdType.MESH
BF, F32 = jnp.bfloat16, jnp.float32

NX, NZ, NY = 4, 8, 4
NROW = 8
MOM = 48
GRID = 1024
LANE = 128
NB = 20
HALF = 5
HROW = HALF * MOM
COLS = NB * MOM
MID = COLS // 2
ROWS = 2 * COLS
SH = 64
PAD = 4 * SH
WIN = 4
NWIN = NB // WIN


def kernel(code_ref, rad_ref, form_hbm, green_ref, kmat_ref, born_hbm,
           v_out, first_out, share_out,
           sign, table, form_ref, colp, rowp, mid, vbuf, vturn, gb_ref, weighted, pown, psend, precv, ssum, zsend, zrecv,
           born_ref, bornp, bturn, vsum, fi, yshard, upd, t32, t16, pbuf, txrecv, tz32, tzsend, tzrecv,
           s1_s, s1_r, s2_s, s2_r, y_s, y_r, z_s, z_r, x_s, x_r, p_s, p_r, r_s, r_r, a_s, a_r, u_s, u_r, f_s, f_r,
           fz_s, fz_r, fx_s, fx_r, tx_s, tx_r, tz_s, tz_r, in_s, out_s):
    row = lax.axis_index("row")
    col = lax.axis_index("col")
    x, z = col // NZ, col % NZ
    y, core = row // 2, row % 2

    def at_x(d):
        return (row, lax.rem(x + d, NX) * NZ + z)

    def at_z(d):
        return (row, x * NZ + lax.rem(z + d, NZ))

    def at_y(d):
        return (lax.rem(y + d, NY) * 2 + core, col)

    sibling = (y * 2 + 1 - core, col)
    in_slab = col < 2 * NROW

    def shift(r, xs):
        k = lax.rem(r // 2 + 2 * xs, 4)
        return jnp.where(lax.rem(r, 2) == 0, k, jnp.where(k == 0, 4, 8 - k))

    def s2_to(xs):
        return 4 * xs + z // 2, lax.rem(z + shift(row, xs), NZ)

    def s2_self(xs):
        to_row, to_z = s2_to(xs)
        return (to_row == row) & (to_z == z)

    def s2_from(half):
        xs, zs = row // 4, lax.rem(2 * row + half, NZ)
        s = lax.rem(z - zs + NZ, NZ)
        k = lax.rem(jnp.minimum(s, NZ - s) + 2 * xs, 4)
        return 2 * k + (s >= 4).astype(jnp.int32), zs

    def s2_from_self(half):
        r, zs = s2_from(half)
        return (r == row) & (zs == z)

    part = col % 2

    def use_col(from_y):
        return from_y // 2 * NZ + 4 * lax.rem(from_y, 2) + 2 * core + z // 4

    home = in_slab & ((col // 2) % 2 == core)

    def copy(src, dst, ss, rs, dev):
        return pltpu.make_async_remote_copy(src_ref=src, dst_ref=dst, send_sem=ss, recv_sem=rs,
                                            device_id=dev, device_id_type=MESH)

    loads = [pltpu.make_async_copy(form_hbm, form_ref, in_s.at[0]), pltpu.make_async_copy(born_hbm, born_ref, in_s.at[1])]
    for c in loads:
        c.start()

    bar = pltpu.get_barrier_semaphore()

    def greet(dev):
        pl.semaphore_signal(bar, inc=1, device_id=dev, device_id_type=MESH)

    for d in range(1, NZ):
        greet(at_z(d))
    for d in range(1, NX):
        greet(at_x(d))
    for d in range(1, NY):
        greet(at_y(d))
    greet(sibling)
    for half in range(2):
        @pl.when(jnp.logical_not(s2_from_self(half)))
        def _():
            r, zs = s2_from(half)
            greet((r, x * NZ + zs))

    @pl.when(home)
    def _():
        def hello(k, carry):
            xx, zz = k // 4, 4 * part + lax.rem(k, 4)

            @pl.when(xx * NZ + zz != col)
            def _():
                greet((row, xx * NZ + zz))
            return carry

        lax.fori_loop(0, 16, hello, 0)

    for k in range(8):
        sign[k] = jnp.float32((1.0 - 2.0 * (k // 4)) / (1.0 + k % 4))
    colp[:, COLS:, :] = jnp.zeros((NROW, 1024 - COLS, LANE), BF)
    for half in range(2):
        edge = slice(half * PAD + HROW, (half + 1) * PAD)
        zsend[edge, :] = jnp.zeros((PAD - HROW, LANE), BF)
        ssum[edge, :] = jnp.zeros((PAD - HROW, LANE), F32)
        bornp[edge, :] = jnp.zeros((PAD - HROW, LANE), F32)
    t32[:, 60:, :] = jnp.zeros((NX * NZ, 4, LANE), F32)

    for b in range(NB):
        gb_ref[b * MOM:(b + 1) * MOM, :] = jnp.broadcast_to(green_ref[b:b + 1, :], (LANE, MOM)).T
    weighted[...] = (gb_ref[...] * kmat_ref[...].astype(F32)).astype(BF)

    def spread(i, carry):
        table[i] = jnp.broadcast_to(form_ref[pl.ds(i, 1), :], (16, GRID)).astype(BF)
        return carry

    loads[0].wait()
    lax.fori_loop(0, 128, spread, 0, unroll=4)

    n_wait = 7 + 3 + 3 + 1 + 4 + 2
    for from_y in range(NY):
        n_wait = n_wait - (use_col(from_y) == col).astype(jnp.int32)
    for xs in range(2):
        n_wait = n_wait - s2_self(xs).astype(jnp.int32)
    pl.semaphore_wait(bar, n_wait)

    def s1_copy(d):
        g = lax.rem(x + d, NX)
        src = rad_ref.at[pl.ds(pl.multiple_of(g * HROW, HROW), HROW)]
        return copy(src, mid.at[x], s1_s.at[d], s1_r.at[x], at_x(d))

    @pl.when(in_slab)
    def _():
        for d in (2, 1, 3):
            s1_copy(d).start()
        mid[x] = rad_ref[pl.ds(pl.multiple_of(x * HROW, HROW), HROW), :]

    below, above = lax.rem(y + 3, NY) * 2 + core, lax.rem(y + 1, NY) * 2 + core
    across = lax.rem(y + 2, NY) * 2 + core
    lo, hi = pl.ds(0, MID), pl.ds(MID, MID)

    def y_copy(k, src, dst, dev):
        return copy(src, dst, y_s.at[k], y_r.at[k], dev)

    def y_part(k, r, part_, dev):
        return y_copy(k, colp.at[r, part_], colp.at[r, part_], dev)

    ys = [
        y_copy(0, rad_ref.at[lo], colp.at[row, lo], at_y(1)),
        y_copy(1, rad_ref.at[hi], colp.at[row, hi], at_y(3)),
        y_copy(2, rad_ref.at[hi], colp.at[row, hi], at_y(1)),
        y_copy(3, rad_ref.at[lo], colp.at[row, lo], at_y(3)),
        y_copy(4, rad_ref, colp.at[row, pl.ds(0, COLS)], sibling),
        y_part(5, below, lo, at_y(1)),
        y_part(6, above, hi, at_y(3)),
        y_part(7, below, lo, sibling),
        y_part(8, above, hi, sibling),
        y_part(9, below, hi, sibling),
        y_part(10, above, lo, sibling),
        y_part(11, across, lo, sibling),
        y_part(12, across, hi, sibling),
    ]
    for k in range(5):
        ys[k].start()
    colp[row, 0:COLS, :] = rad_ref[...]

    def s2_copy(xs):
        to_row, to_z = s2_to(xs)
        half = lax.rem(z, 2)
        return copy(mid.at[xs], rowp.at[x, half, to_z], s2_s.at[xs], s2_r.at[half], (to_row, x * NZ + to_z))

    for xs in range(2):
        @pl.when(x != xs)
        def _():
            copy(mid.at[xs], mid.at[xs], s1_s.at[0], s1_r.at[xs], sibling).wait_recv()

        @pl.when(s2_self(xs))
        def _():
            rowp[x, lax.rem(z, 2), z] = mid[xs]

        @pl.when(jnp.logical_not(s2_self(xs)))
        def _():
            s2_copy(xs).start()

    def flow_at(f):
        if f == 0:
            return x, 0
        return lax.rem(x + f - 1, NX), 1

    def steps(f, sign):
        return 4 if (f <= 2) == (sign > 0) else 3

    def z_copy(f, sign, s):
        g, half = flow_at(f)
        origin = lax.rem(z + (NZ - s if sign > 0 else s), NZ)
        k = (f * 2 + (0 if sign > 0 else 1)) * 4 + s
        ref = rowp.at[g, half, origin]
        return copy(ref, ref, z_s.at[k], z_r.at[k], at_z(1 if sign > 0 else NZ - 1))

    def z_wait(f, sign, s):
        z_copy(f, sign, s).wait_recv()
        if s + 1 < steps(f, sign):
            z_copy(f, sign, s + 1).start()

    def piece(k):
        d = (k + 1) // 2
        return lax.rem(z + (NZ - d if k % 2 == 1 else d), NZ)

    def xh2(k, sign):
        ref = rowp.at[x, 0, piece(k)]
        n = k if sign > 0 else 8 + k
        return copy(ref, ref, x_s.at[n], x_r.at[n], at_x(1 if sign > 0 else 3))

    def xh2_forward(k):
        sign = 1 if k % 2 == 0 else -1
        ref = rowp.at[lax.rem(x + (3 if sign > 0 else 1), NX), 0, piece(k)]
        return copy(ref, ref, x_s.at[16 + k], x_r.at[16 + k], at_x(1 if sign > 0 else 3))

    def xh2_start(k):
        xh2(k, 1).start()
        xh2(k, -1).start()

    def xh2_wait(k):
        xh2(k, 1).wait_recv()
        xh2(k, -1).wait_recv()
        xh2_forward(k).start()

    def xh1(n):
        ref = rowp.at[lax.rem(x + (3 if n == 2 else 0), NX), 1, z]
        return copy(ref, ref, x_s.at[24 + n], x_r.at[24 + n], at_x(3 if n == 1 else 1))

    def flow_start(f):
        z_copy(f, 1, 0).start()
        z_copy(f, -1, 0).start()

    def sc_wait(half):
        @pl.when(jnp.logical_not(s2_from_self(half)))
        def _():
            ref = rowp.at[x, half, z]
            copy(ref, ref, s2_s.at[0], s2_r.at[half], sibling).wait_recv()

    sc_wait(0)
    flow_start(0)
    xh2_start(0)
    sc_wait(1)
    flow_start(1)
    xh1(0).start()
    xh1(1).start()

    def y_on(k, *then):
        ys[k].wait_recv()
        for n in then:
            ys[n].start()

    y_on(0, 5, 7)
    y_on(1, 6, 8)
    lax.fori_loop(128, 192, spread, 0, unroll=4)
    y_on(2, 9)
    y_on(3, 10)

    def own_step(s_):
        for sign_ in (1, -1):
            if s_ < steps(0, sign_):
                z_wait(0, sign_, s_)
                xh2_start(2 * s_ + (1 if sign_ > 0 else 2))
        for sign_ in (1, -1):
            if s_ < steps(1, sign_):
                z_wait(1, sign_, s_)

    def others(s_, *flows):
        for f in flows:
            for sign_ in (1, -1):
                if s_ < steps(f, sign_):
                    z_wait(f, sign_, s_)

    def part_0():
        own_step(0)
        lax.fori_loop(192, 256, spread, 0, unroll=4)
        y_on(5, 11)
        y_on(6, 12)
        xh1(0).wait_recv()
        xh1(2).start()
        flow_start(4)
        xh1(1).wait_recv()
        flow_start(2)
        xh2_wait(0)
        for k in (4, 7, 8, 9, 10, 11, 12):
            ys[k].wait_recv()

    def part_1():
        own_step(1)
        xh1(2).wait_recv()
        flow_start(3)
        others(0, 4, 2)
        xh2_wait(1)
        xh2_wait(2)

    def part_2():
        own_step(2)
        xh2_wait(3)
        xh2_wait(4)
        loads[1].wait()
        for half in range(2):
            bornp[half * PAD:half * PAD + HROW, :] = born_ref[pl.ds(pl.multiple_of(half * COLS + x * HROW, HROW), HROW), :]

    def part_3():
        own_step(3)
        others(1, 4, 2)
        others(0, 3)
        xh2_wait(5)
        xh2_wait(6)

    def before_2():
        xh2_wait(7)

    def before_3():
        others(2, 4, 2)
        others(1, 3)

    def before_4():
        for k in range(8):
            xh2_forward(k).wait_recv()

    def before_5():
        z_wait(2, 1, 3)
        others(2, 3)

    def before_6():
        z_wait(4, -1, 3)

    def before_7():
        z_wait(3, -1, 3)

    parts_before = {0: part_0, 1: part_1, 2: part_2, 3: part_3}
    befores = {2: before_2, 3: before_3, 4: before_4, 5: before_5, 6: before_6, 7: before_7}

    def p_copy(d, half):
        n = (d - 1) * 2 + half
        return copy(psend.at[n], precv.at[n], p_s.at[n], p_r.at[n], at_x(d))

    def batch(t):
        third = lax.rem(t - 2, 3)
        d = jnp.where(third == 0, 1, jnp.where(third == 1, 3, 2))
        half = jnp.where(t >= 5, 1, 0)
        return d, lax.rem(x + d, NX), half

    lanes = lax.broadcasted_iota(jnp.int32, (MOM, 256), 1)

    def grid_part(half, slot_):
        step = lax.rem(slot_ - lax.rem(2 * row + half, NZ) + NZ, NZ)
        k = lax.rem(jnp.minimum(step, NZ - step) + 2 * (row // 4), 4)
        return 2 * k + (step >= 4).astype(jnp.int32)

    def products(g, half, chunks, put):
        first = half * NB + g * HALF
        for w in range(NWIN):
            base = w * WIN * MOM
            start = base // LANE * LANE
            off = base - start
            win = jnp.concatenate([colp[r, start:start + 256, :] for _, r in chunks], axis=1)
            parts = []
            for i in range(HALF):
                chan = jnp.concatenate([rowp[g, half, c, i * MOM:(i + 1) * MOM, :] for c, _ in chunks], axis=1)
                chan = chan.reshape(3, 16, len(chunks) * LANE)
                for j in range(WIN):
                    which = code_ref[w * WIN + j, first + i] & 255
                    if len(chunks) == NROW:
                        factor = table[which]
                    else:
                        factor = jnp.concatenate(
                            [table[which, :, pl.ds(pl.multiple_of(r * LANE, LANE), LANE)] for _, r in chunks], axis=1)
                    parts.append((chan * factor[None]).reshape(MOM, len(chunks) * LANE))
            scaled = jnp.concatenate(parts, axis=0)
            prod = lax.dot_general(scaled, win, (((1,), (1,)), ((), ())), preferred_element_type=F32)
            for i in range(HALF):
                acc = jnp.zeros((MOM, 256), F32)
                for j in range(WIN):
                    n = i * WIN + j
                    low = off + j * MOM
                    mine = prod[n * MOM:(n + 1) * MOM] * sign[code_ref[w * WIN + j, first + i] >> 8]
                    acc = jnp.where((lanes >= low) & (lanes < low + MOM), mine, acc)
                put(i, start, off, acc)

    def batch_rows(g, half):
        return pl.ds(pl.multiple_of((half * NB + g * HALF) * MOM, HROW), HROW)

    vsum[...] = jnp.zeros((2, HROW, 1024), F32)

    def own_part(p, carry):
        for k, fn in parts_before.items():
            pl.when(p == k)(fn)

        def place(k):
            d = (k + 1) // 2
            return lax.rem(jnp.where(lax.rem(k, 2) == 1, z + NZ - d, z + d), NZ)

        def one(half, carry_):
            chunks = []
            for k in (2 * p, 2 * p + 1):
                chunks.append((place(k), grid_part(half, place(k))))

            def put(i, start, off, acc):
                vsum[half, i * MOM:(i + 1) * MOM, start:start + 256] += acc

            products(x, half, chunks, put)
            return carry_

        return lax.fori_loop(0, 2, one, carry)

    lax.fori_loop(0, 4, own_part, 0)
    for half in range(2):
        vbuf[batch_rows(x, half), :] = vsum[half, :, 0:COLS].astype(BF)
        pown[half] = jnp.dot(vbuf[batch_rows(x, half), :], weighted[...], preferred_element_type=F32)

    def build(t, carry):
        for k, fn in befores.items():
            pl.when(t == k)(fn)
        d, g, half = batch(t)
        zs = lax.rem(2 * row + half, NZ)
        chunks = [(lax.rem(zs + shift(jnp.int32(r), row // 4), NZ), r) for r in range(NROW)]

        def put(i, start, off, acc):
            rows = pl.ds(pl.multiple_of((half * NB + g * HALF + i) * MOM, MOM), MOM)
            width = min(256, COLS - start)
            new = acc.astype(BF)
            if off:
                new = jnp.where(lanes >= off, new, vbuf[rows, start:start + width])
            vbuf[rows, start:start + width] = new[:, :width]

        products(g, half, chunks, put)
        part_sum = jnp.dot(vbuf[batch_rows(g, half), :], weighted[...], preferred_element_type=F32)
        psend[(d - 1) * 2 + half] = part_sum.astype(BF)
        p_copy(d, half).start()
        return carry

    lax.fori_loop(2, 8, build, 0)

    def tx_copy(d):
        to = lax.rem(x + d, NX)
        return copy(t16.at[pl.ds(to * NZ, NZ)], txrecv.at[d - 1], tx_s.at[d], tx_r.at[d], at_x(d))

    def second(operand):
        turned = operand.T.astype(BF)

        def chunk(q, carry):
            rows = pl.ds(pl.multiple_of(q * 384, 384), 384)
            prod = lax.dot_general(turned, vbuf[rows, :], (((1,), (1,)), ((), ())), preferred_element_type=F32)
            for jj in range(3):
                pbuf[jj] = prod[:, jj * LANE:(jj + 1) * LANE]
            for jj in range(3):
                for c in range(NX * NZ):
                    t32[c, pl.ds(q * 12 + jj * 4, 4), :] = pbuf[jj, 4 * c:4 * c + 4, :]
            return carry

        lax.fori_loop(0, 5, chunk, 0)
        t16[...] = t32[...].astype(BF)
        for d in (2, 1, 3):
            tx_copy(d).start()

    def turn(m, carry):
        at = pl.ds(pl.multiple_of(m * LANE, LANE), LANE)
        vturn[:, at] = vbuf[at, :].T
        return carry

    @pl.when(jnp.logical_not(in_slab))
    def _():
        second(weighted[...].astype(F32))

    for n in range(6):
        p_copy(n // 2 + 1, n % 2).wait_recv()
    for half in range(2):
        total = pown[half]
        for d in range(3):
            total = total + precv[d * 2 + half].astype(F32)
        ssum[half * PAD:half * PAD + HROW, :] = total
        zsend[half * PAD:half * PAD + HROW, :] = total.astype(BF)

    def shard(q):
        return pl.ds(pl.multiple_of(q * SH, SH), SH)

    def r_copy(d):
        return copy(zsend.at[shard(lax.rem(z + d, NZ))], zrecv.at[d - 1], r_s.at[d], r_r.at[d], at_z(d))

    for d in range(1, NZ):
        r_copy(d).start()
    lax.fori_loop(0, 4, turn, 0)
    for d in range(1, NZ):
        r_copy(d).wait_recv()
    total = bornp[shard(z), :] + ssum[shard(z), :]
    for d in range(NZ - 1):
        total = total + zrecv[d].astype(F32)
    fresh = total.astype(BF)
    fi[x, shard(z), :] = fresh
    yshard[y] = fresh

    def a_copy(d):
        return copy(yshard.at[y], yshard.at[y], a_s.at[d], a_r.at[d], at_y(d))

    for d in (2, 1, 3):
        a_copy(d).start()

    def u_copy(d):
        from_y = lax.rem(y + d, NY)
        return copy(yshard.at[from_y], upd.at[x, shard(lax.rem(z, 4))], u_s.at[d], u_r.at[x * 4 + lax.rem(z, 4)],
                    (row, use_col(from_y)))

    def u_self(d):
        return use_col(lax.rem(y + d, NY)) == col

    for d in (0, 1, 3, 2):
        if d > 0:
            from_y = lax.rem(y + d, NY)
            copy(yshard.at[from_y], yshard.at[from_y], a_s.at[d], a_r.at[NY - d], at_y(d)).wait_recv()

        @pl.when(u_self(d))
        def _():
            upd[x, shard(lax.rem(z, 4)), :] = yshard[lax.rem(y + d, NY)]

        @pl.when(jnp.logical_not(u_self(d)))
        def _():
            u_copy(d).start()

    def fz_copy(d):
        ref = fi.at[x, shard(z)]
        return copy(ref, ref, fz_s.at[d], fz_r.at[d], at_z(d))

    for d in range(1, NZ):
        fz_copy(d).start()

    def f_copy(g):
        ref = upd.at[g, pl.ds(0, HROW)]
        return copy(ref, ref, f_s.at[g], f_r.at[g], sibling)

    lax.fori_loop(4, 8, turn, 0)

    @pl.when(home)
    def _():
        for g in range(NX):
            for q in range(4):
                @pl.when(g * NZ + 4 * part + q != col)
                def _():
                    ref = upd.at[g, pl.ds(q * SH, SH)]
                    copy(ref, ref, u_s.at[0], u_r.at[g * 4 + q], sibling).wait_recv()
            f_copy(g).start()

    @pl.when(in_slab)
    def _():
        @pl.when(jnp.logical_not(home))
        def _():
            for g in range(NX):
                f_copy(g).wait_recv()
        fresh_rows = jnp.concatenate([upd[g, 0:HROW, :] for g in range(NX)], axis=0)
        second((gb_ref[...] * fresh_rows.astype(F32)).astype(BF).astype(F32))

    for d in range(1, NZ):
        ref = fi.at[x, shard(lax.rem(z + NZ - d, NZ))]
        copy(ref, ref, fz_s.at[d], fz_r.at[d], at_z(d)).wait_recv()

    def fx_copy(d, g):
        return copy(fi.at[g], fi.at[g], fx_s.at[d], fx_r.at[d], at_x(d))

    for d in (2, 1, 3):
        fx_copy(d, x).start()

    lax.fori_loop(8, 15, turn, 0)

    def v_copy():
        return pltpu.make_async_copy(vturn, v_out, out_s.at[8])

    v_copy().start()
    for j in range(15):
        bturn[j] = born_ref[j * LANE:(j + 1) * LANE, :].T

    for d in range(1, NX):
        tx_copy(d).wait_recv()
    total = t32[pl.ds(x * NZ, NZ)]
    for d in range(NX - 1):
        total = total + txrecv[d].astype(F32)
    tz32[...] = total
    tzsend[...] = total.astype(BF)

    def tz_copy(d):
        return copy(tzsend.at[lax.rem(z + d, NZ)], tzrecv.at[d - 1], tz_s.at[d], tz_r.at[d], at_z(d))

    for d in range(1, NZ):
        tz_copy(d).start()
    for d in range(1, NX):
        fx_copy(d, lax.rem(x + NX - d, NX)).wait_recv()

    def f_out(g, half):
        return pltpu.make_async_copy(fi.at[g, pl.ds(half * PAD, HROW)],
                                     first_out.at[pl.ds(half * COLS + g * HROW, HROW)], out_s.at[2 * g + half])

    for g in range(NX):
        for half in range(2):
            f_out(g, half).start()
    for d in range(1, NZ):
        tz_copy(d).wait_recv()
    total = tz32[z]
    for d in range(NZ - 1):
        total = total + tzrecv[d].astype(F32)
    tz32[z] = total
    for j in range(15):
        share_out[:, j * LANE:(j + 1) * LANE] = tz32[z, 4 * j:4 * j + 4, :] + bturn[j, pl.ds(4 * col, 4), :]

    for g in range(NX):
        for half in range(2):
            f_out(g, half).wait()
    v_copy().wait()

    @pl.when(in_slab)
    def _():
        for d in range(1, NX):
            s1_copy(d).wait_send()

    for xs in range(2):
        @pl.when(jnp.logical_not(s2_self(xs)))
        def _():
            s2_copy(xs).wait_send()
    for c in ys:
        c.wait_send()
    for f in range(5):
        for sign in (1, -1):
            for s in range(steps(f, sign)):
                z_copy(f, sign, s).wait_send()
    for k in range(8):
        xh2(k, 1).wait_send()
        xh2(k, -1).wait_send()
        xh2_forward(k).wait_send()
    for n in range(3):
        xh1(n).wait_send()
    for n in range(6):
        p_copy(n // 2 + 1, n % 2).wait_send()
    for d in range(1, NZ):
        r_copy(d).wait_send()
        fz_copy(d).wait_send()
        tz_copy(d).wait_send()
    for d in range(1, NX):
        fx_copy(d, x).wait_send()
        tx_copy(d).wait_send()

    for d in range(1, NY):
        a_copy(d).wait_send()
    for d in range(NY):
        @pl.when(jnp.logical_not(u_self(d)))
        def _():
            u_copy(d).wait_send()

    @pl.when(home)
    def _():
        for g in range(NX):
            f_copy(g).wait_send()


def hand_over(v_in, f_in, s_in, v_out, f_out, s_out, v_mid, f_mid, s_mid, sem):
    trips = [(f_in, f_mid, f_out), (s_in, s_mid, s_out)]
    for q in range(6):
        rows = pl.ds(q * 160, 160)
        trips.append((v_in.at[rows], v_mid.at[rows], v_out.at[rows]))
    there = [pltpu.make_async_copy(src, mid, sem.at[n]) for n, (src, mid, _) in enumerate(trips)]
    back = [pltpu.make_async_copy(mid, dst, sem.at[8 + n]) for n, (_, mid, dst) in enumerate(trips)]
    for c in there:
        c.start()
    for c, d in zip(there, back):
        c.wait()
        d.start()
    for c in back:
        c.wait()


def body(radial, form_factors, coupling, quantum, green_diag, kmatrix, born_term):
    row_count, col_count = coupling.shape
    row_index, col_index = lax.axis_index("row"), lax.axis_index("col")
    rq = lax.dynamic_slice_in_dim(quantum, row_index * row_count, row_count, 0)
    cq = lax.dynamic_slice_in_dim(quantum, col_index * col_count, col_count, 0)
    table_index = coupling * (NTARG * NTARG) + rq[:, 2:3] * NTARG + cq[:, 2][None, :]
    parity = (rq[:, 0:1] + cq[:, 0][None, :]) % 2
    spread_m = jnp.abs(rq[:, 1:2] - cq[:, 1][None, :])
    code = (table_index + 256 * (4 * parity + spread_m)).T
    vm = pl.BlockSpec(memory_space=pltpu.VMEM)
    sm = pl.BlockSpec(memory_space=pltpu.SMEM)
    hb = pl.BlockSpec(memory_space=pl.ANY)
    dma = pltpu.SemaphoreType.DMA
    v_block, first, share = pl.pallas_call(
        kernel,
        out_shape=(
            jax.ShapeDtypeStruct((COLS, ROWS), BF),
            jax.ShapeDtypeStruct((ROWS, LANE), BF),
            jax.ShapeDtypeStruct((4, ROWS), F32),
        ),
        in_specs=[sm, vm, hb, vm, vm, hb],
        out_specs=(hb, hb, vm),
        scratch_shapes=[
            pltpu.SMEM((8,), F32),
            pltpu.VMEM((256, 16, GRID), BF),
            pltpu.VMEM((256, GRID), F32),
            pltpu.VMEM((NROW, 1024, LANE), BF),
            pltpu.VMEM((NX, 2, NROW, HROW, LANE), BF),
            pltpu.VMEM((2, HROW, LANE), BF),
            pltpu.VMEM((ROWS, COLS), BF),
            pltpu.VMEM((COLS, ROWS), BF),
            pltpu.VMEM((COLS, LANE), F32),
            pltpu.VMEM((COLS, LANE), BF),
            pltpu.VMEM((2, HROW, LANE), F32),
            pltpu.VMEM((6, HROW, LANE), BF),
            pltpu.VMEM((6, HROW, LANE), BF),
            pltpu.VMEM((2 * PAD, LANE), F32),
            pltpu.VMEM((2 * PAD, LANE), BF),
            pltpu.VMEM((NZ - 1, SH, LANE), BF),
            pltpu.VMEM((ROWS, LANE), F32),
            pltpu.VMEM((2 * PAD, LANE), F32),
            pltpu.VMEM((15, LANE, LANE), F32),
            pltpu.VMEM((2, HROW, 1024), F32),
            pltpu.VMEM((NX, 2 * PAD, LANE), BF),
            pltpu.VMEM((NY, SH, LANE), BF),
            pltpu.VMEM((NX, PAD, LANE), BF),
            pltpu.VMEM((NX * NZ, SH, LANE), F32),
            pltpu.VMEM((NX * NZ, SH, LANE), BF),
            pltpu.VMEM((3, LANE, LANE), F32),
            pltpu.VMEM((NX - 1, NZ, SH, LANE), BF),
            pltpu.VMEM((NZ, SH, LANE), F32),
            pltpu.VMEM((NZ, SH, LANE), BF),
            pltpu.VMEM((NZ - 1, SH, LANE), BF),
            dma((4,)), dma((2,)), dma((2,)), dma((2,)), dma((13,)), dma((13,)), dma((40,)), dma((40,)), dma((27,)), dma((27,)),
            dma((6,)), dma((6,)), dma((8,)), dma((8,)), dma((4,)), dma((4,)), dma((4,)), dma((16,)), dma((4,)), dma((4,)),
            dma((8,)), dma((8,)), dma((4,)), dma((4,)), dma((4,)), dma((4,)), dma((8,)), dma((8,)), dma((2,)), dma((9,)),
        ],
        compiler_params=pltpu.CompilerParams(collective_id=0, has_side_effects=True, vmem_limit_bytes=58 << 20),
        name="sweeps",
    )(code, radial.reshape(COLS, LANE), form_factors, green_diag, kmatrix, born_term)
    v_block, first, share = pl.pallas_call(
        hand_over,
        out_shape=(
            jax.ShapeDtypeStruct((COLS, ROWS), BF),
            jax.ShapeDtypeStruct((ROWS, LANE), BF),
            jax.ShapeDtypeStruct((4, ROWS), F32),
        ),
        in_specs=[hb, hb, hb],
        out_specs=(hb, hb, hb),
        scratch_shapes=[pltpu.VMEM((COLS, ROWS), BF), pltpu.VMEM((ROWS, LANE), BF), pltpu.VMEM((4, ROWS), F32), dma((16,))],
        name="hand_over",
    )(v_block, first, share)
    return v_block.T, first, share.T


def solution(mesh):
    placed = (
        P("col", None, "row"),
        P(),
        P("row", "col"),
        P(),
        P("col", None),
        P("col", None),
        P("row", None),
    )
    return jax.shard_map(
        body,
        mesh=mesh,
        in_specs=placed,
        out_specs=(P("row", "col"), P("row", None), P("row", "col")),
        check_vma=False,
    )
```

```python
import functools

import jax
import jax.numpy as jnp
from jax import lax
from jax.experimental import pallas as pl
from jax.experimental.pallas import tpu as pltpu
from jax.sharding import PartitionSpec as P

NTARG = 4
MESH = pl.DeviceIdType.MESH
BF, F32 = jnp.bfloat16, jnp.float32

NX, NZ, NY = 4, 8, 4
NROW = 8
MOM = 48
GRID = 1024
LANE = 128
NB = 20
HALF = 5
HROW = HALF * MOM
COLS = NB * MOM
MID = COLS // 2
ROWS = 2 * COLS
SH = 64
PAD = 4 * SH
WIN = 4
NWIN = NB // WIN


def kernel(code_ref, rad_ref, form_hbm, green_ref, kmat_ref, born_hbm,
           v_out, first_out, share_out,
           sign, table, form_ref, colp, rowp, mid, vbuf, vturn, gb_ref, weighted, pown, psend, precv, ssum, zsend, zrecv,
           born_ref, bornp, bturn, vsum, fi, yshard, upd, t32, t16, pbuf, txrecv, tz32, tzsend, tzrecv,
           s1_s, s1_r, s2_s, s2_r, y_s, y_r, z_s, z_r, x_s, x_r, p_s, p_r, r_s, r_r, a_s, a_r, u_s, u_r, f_s, f_r,
           fz_s, fz_r, fx_s, fx_r, tx_s, tx_r, tz_s, tz_r, in_s, out_s):
    row = lax.axis_index("row")
    col = lax.axis_index("col")
    x, z = col // NZ, col % NZ
    y, core = row // 2, row % 2

    def at_x(d):
        return (row, lax.rem(x + d, NX) * NZ + z)

    def at_z(d):
        return (row, x * NZ + lax.rem(z + d, NZ))

    def at_y(d):
        return (lax.rem(y + d, NY) * 2 + core, col)

    sibling = (y * 2 + 1 - core, col)
    in_slab = col < 2 * NROW

    def shift(r, xs):
        k = lax.rem(r // 2 + 2 * xs, 4)
        return jnp.where(lax.rem(r, 2) == 0, k, jnp.where(k == 0, 4, 8 - k))

    def s2_to(xs):
        return 4 * xs + z // 2, lax.rem(z + shift(row, xs), NZ)

    def s2_self(xs):
        to_row, to_z = s2_to(xs)
        return (to_row == row) & (to_z == z)

    def s2_from(half):
        xs, zs = row // 4, lax.rem(2 * row + half, NZ)
        s = lax.rem(z - zs + NZ, NZ)
        k = lax.rem(jnp.minimum(s, NZ - s) + 2 * xs, 4)
        return 2 * k + (s >= 4).astype(jnp.int32), zs

    def s2_from_self(half):
        r, zs = s2_from(half)
        return (r == row) & (zs == z)

    part = col % 2

    def use_col(from_y):
        return from_y // 2 * NZ + 4 * lax.rem(from_y, 2) + 2 * core + z // 4

    home = in_slab & ((col // 2) % 2 == core)

    def copy(src, dst, ss, rs, dev):
        return pltpu.make_async_remote_copy(src_ref=src, dst_ref=dst, send_sem=ss, recv_sem=rs,
                                            device_id=dev, device_id_type=MESH)

    loads = [pltpu.make_async_copy(form_hbm, form_ref, in_s.at[0]), pltpu.make_async_copy(born_hbm, born_ref, in_s.at[1])]
    for c in loads:
        c.start()

    bar = pltpu.get_barrier_semaphore()

    def greet(dev):
        pl.semaphore_signal(bar, inc=1, device_id=dev, device_id_type=MESH)

    for d in range(1, NZ):
        greet(at_z(d))
    for d in range(1, NX):
        greet(at_x(d))
    for d in range(1, NY):
        greet(at_y(d))
    greet(sibling)
    for half in range(2):
        @pl.when(jnp.logical_not(s2_from_self(half)))
        def _():
            r, zs = s2_from(half)
            greet((r, x * NZ + zs))

    @pl.when(home)
    def _():
        def hello(k, carry):
            xx, zz = k // 4, 4 * part + lax.rem(k, 4)

            @pl.when(xx * NZ + zz != col)
            def _():
                greet((row, xx * NZ + zz))
            return carry

        lax.fori_loop(0, 16, hello, 0)

    n_wait = 7 + 3 + 3 + 1 + 4 + 2
    for from_y in range(NY):
        n_wait = n_wait - (use_col(from_y) == col).astype(jnp.int32)
    for xs in range(2):
        n_wait = n_wait - s2_self(xs).astype(jnp.int32)
    pl.semaphore_wait(bar, n_wait)

    def s1_copy(d):
        g = lax.rem(x + d, NX)
        src = rad_ref.at[pl.ds(pl.multiple_of(g * HROW, HROW), HROW)]
        return copy(src, mid.at[x], s1_s.at[d], s1_r.at[x], at_x(d))

    @pl.when(in_slab)
    def _():
        for d in (2, 1, 3):
            s1_copy(d).start()
        mid[x] = rad_ref[pl.ds(pl.multiple_of(x * HROW, HROW), HROW), :]

    below, above = lax.rem(y + 3, NY) * 2 + core, lax.rem(y + 1, NY) * 2 + core
    across = lax.rem(y + 2, NY) * 2 + core
    lo, hi = pl.ds(0, MID), pl.ds(MID, MID)

    def y_copy(k, src, dst, dev):
        return copy(src, dst, y_s.at[k], y_r.at[k], dev)

    def y_part(k, r, part_, dev):
        return y_copy(k, colp.at[r, part_], colp.at[r, part_], dev)

    ys = [
        y_copy(0, rad_ref.at[lo], colp.at[row, lo], at_y(1)),
        y_copy(1, rad_ref.at[hi], colp.at[row, hi], at_y(3)),
        y_copy(2, rad_ref.at[hi], colp.at[row, hi], at_y(1)),
        y_copy(3, rad_ref.at[lo], colp.at[row, lo], at_y(3)),
        y_copy(4, rad_ref, colp.at[row, pl.ds(0, COLS)], sibling),
        y_part(5, below, lo, at_y(1)),
        y_part(6, above, hi, at_y(3)),
        y_part(7, below, lo, sibling),
        y_part(8, above, hi, sibling),
        y_part(9, below, hi, sibling),
        y_part(10, above, lo, sibling),
        y_part(11, across, lo, sibling),
        y_part(12, across, hi, sibling),
    ]
    for k in range(5):
        ys[k].start()
    colp[row, 0:COLS, :] = rad_ref[...]

    def spread(i, carry):
        table[i] = jnp.broadcast_to(form_ref[pl.ds(i, 1), :], (16, GRID)).astype(BF)
        return carry

    loads[0].wait()
    lax.fori_loop(0, 64, spread, 0, unroll=4)

    def s2_copy(xs):
        to_row, to_z = s2_to(xs)
        half = lax.rem(z, 2)
        return copy(mid.at[xs], rowp.at[x, half, to_z], s2_s.at[xs], s2_r.at[half], (to_row, x * NZ + to_z))

    def s2_start(xs):
        @pl.when(s2_self(xs))
        def _():
            rowp[x, lax.rem(z, 2), z] = mid[xs]

        @pl.when(jnp.logical_not(s2_self(xs)))
        def _():
            s2_copy(xs).start()

    @pl.when(in_slab)
    def _():
        s2_start(x)

    for xs in range(2):
        @pl.when(x != xs)
        def _():
            copy(mid.at[xs], mid.at[xs], s1_s.at[0], s1_r.at[xs], sibling).wait_recv()
            s2_start(xs)

    for k in range(8):
        sign[k] = jnp.float32((1.0 - 2.0 * (k // 4)) / (1.0 + k % 4))
    colp[:, COLS:, :] = jnp.zeros((NROW, 1024 - COLS, LANE), BF)
    for half in range(2):
        edge = slice(half * PAD + HROW, (half + 1) * PAD)
        zsend[edge, :] = jnp.zeros((PAD - HROW, LANE), BF)
        ssum[edge, :] = jnp.zeros((PAD - HROW, LANE), F32)
        bornp[edge, :] = jnp.zeros((PAD - HROW, LANE), F32)
    t32[:, 60:, :] = jnp.zeros((NX * NZ, 4, LANE), F32)

    for b in range(NB):
        gb_ref[b * MOM:(b + 1) * MOM, :] = jnp.broadcast_to(green_ref[b:b + 1, :], (LANE, MOM)).T
    weighted[...] = (gb_ref[...] * kmat_ref[...].astype(F32)).astype(BF)

    lax.fori_loop(64, 128, spread, 0, unroll=4)

    def flow_at(f):
        if f == 0:
            return x, 0
        return lax.rem(x + f - 1, NX), 1

    def steps(f, sign):
        return 4 if (f in (0, 2)) == (sign > 0) else 3

    def z_copy(f, sign, s):
        g, half = flow_at(f)
        origin = lax.rem(z + (NZ - s if sign > 0 else s), NZ)
        k = (f * 2 + (0 if sign > 0 else 1)) * 4 + s
        ref = rowp.at[g, half, origin]
        return copy(ref, ref, z_s.at[k], z_r.at[k], at_z(1 if sign > 0 else NZ - 1))

    def z_wait(f, sign, s):
        z_copy(f, sign, s).wait_recv()
        if s + 1 < steps(f, sign):
            z_copy(f, sign, s + 1).start()

    def piece(k):
        d = (k + 1) // 2
        return lax.rem(z + (NZ - d if k % 2 == 1 else d), NZ)

    def xh2(k, sign):
        ref = rowp.at[x, 0, piece(k)]
        n = k if sign > 0 else 8 + k
        return copy(ref, ref, x_s.at[n], x_r.at[n], at_x(1 if sign > 0 else 3))

    def xh2_forward(k):
        sign = 1 if k % 2 == 0 else -1
        ref = rowp.at[lax.rem(x + (3 if sign > 0 else 1), NX), 0, piece(k)]
        return copy(ref, ref, x_s.at[16 + k], x_r.at[16 + k], at_x(1 if sign > 0 else 3))

    def xh2_start(k):
        xh2(k, 1).start()
        xh2(k, -1).start()

    def xh2_wait(k):
        xh2(k, 1).wait_recv()
        xh2(k, -1).wait_recv()

    def xh1(n):
        ref = rowp.at[x, 1, z]
        return copy(ref, ref, x_s.at[24 + n], x_r.at[24 + n], at_x(3 if n == 1 else 1))

    def xf(k):
        sign = 1 if k % 2 == 0 else -1
        ref = rowp.at[lax.rem(x + (3 if sign > 0 else 1), NX), 1, piece(k)]
        return copy(ref, ref, x_s.at[26 + k], x_r.at[26 + k], at_x(1 if sign > 0 else 3))

    def flow_start(f):
        z_copy(f, 1, 0).start()
        z_copy(f, -1, 0).start()

    def sc_wait(half):
        @pl.when(jnp.logical_not(s2_from_self(half)))
        def _():
            ref = rowp.at[x, half, z]
            copy(ref, ref, s2_s.at[0], s2_r.at[half], sibling).wait_recv()

    sc_wait(0)
    flow_start(0)
    xh2_start(0)
    sc_wait(1)
    flow_start(1)
    xh1(0).start()
    xh1(1).start()

    def y_on(k, *then):
        ys[k].wait_recv()
        for n in then:
            ys[n].start()

    y_on(0, 5, 7)
    y_on(1, 6, 8)
    lax.fori_loop(128, 192, spread, 0, unroll=4)
    y_on(2, 9)
    y_on(3, 10)

    def own_step(s_):
        for sign_ in (1, -1):
            if s_ < steps(0, sign_):
                z_wait(0, sign_, s_)
                xh2_start(2 * s_ + (1 if sign_ > 0 else 2))
        for sign_ in (1, -1):
            if s_ < steps(1, sign_):
                z_wait(1, sign_, s_)

    def far_step(s_):
        if s_ < 3:
            z_wait(4, 1, s_)
        z_wait(4, -1, s_)
        if s_ < 3:
            xf(2 * s_ + 2).start()
        z_wait(2, 1, s_)
        xf(2 * s_ + 1).start()
        if s_ < 3:
            z_wait(2, -1, s_)

    def part_0():
        own_step(0)
        lax.fori_loop(192, 256, spread, 0, unroll=4)
        y_on(5, 11)
        y_on(6, 12)
        xh1(0).wait_recv()
        xf(0).start()
        flow_start(4)
        xh1(1).wait_recv()
        flow_start(2)
        xh2_wait(0)
        for k in (4, 7, 8, 9, 10, 11, 12):
            ys[k].wait_recv()

    def part_1():
        own_step(1)
        far_step(0)
        xh2_wait(1)
        xh2_wait(2)

    def part_2():
        own_step(2)
        xh2_wait(3)
        xh2_wait(4)
        loads[1].wait()
        for half in range(2):
            bornp[half * PAD:half * PAD + HROW, :] = born_ref[pl.ds(pl.multiple_of(half * COLS + x * HROW, HROW), HROW), :]

    def part_3():
        own_step(3)
        far_step(1)
        xh2_wait(5)
        xh2_wait(6)
        for k in range(7):
            xh2_forward(k).start()

    def before_2():
        xh2_wait(7)
        xh2_forward(7).start()

    def before_3():
        far_step(2)

    def before_4():
        for k in range(8):
            xh2_forward(k).wait_recv()

    def before_5():
        far_step(3)

    def before_6():
        pass

    def before_7():
        for k in range(8):
            xf(k).wait_recv()

    parts_before = {0: part_0, 1: part_1, 2: part_2, 3: part_3}
    befores = {2: before_2, 3: before_3, 4: before_4, 5: before_5, 6: before_6, 7: before_7}

    def p_copy(d, half):
        n = (d - 1) * 2 + half
        return copy(psend.at[n], precv.at[n], p_s.at[n], p_r.at[n], at_x(d))

    def batch(t):
        third = lax.rem(t - 2, 3)
        d = jnp.where(third == 0, 1, jnp.where(third == 1, 3, 2))
        half = jnp.where(t >= 5, 1, 0)
        return d, lax.rem(x + d, NX), half

    lanes = lax.broadcasted_iota(jnp.int32, (MOM, 256), 1)

    def grid_part(half, slot_):
        step = lax.rem(slot_ - lax.rem(2 * row + half, NZ) + NZ, NZ)
        k = lax.rem(jnp.minimum(step, NZ - step) + 2 * (row // 4), 4)
        return 2 * k + (step >= 4).astype(jnp.int32)

    def products(g, half, chunks, put):
        first = half * NB + g * HALF
        for w in range(NWIN):
            base = w * WIN * MOM
            start = base // LANE * LANE
            off = base - start
            win = jnp.concatenate([colp[r, start:start + 256, :] for _, r in chunks], axis=1)
            parts = []
            for i in range(HALF):
                chan = jnp.concatenate([rowp[g, half, c, i * MOM:(i + 1) * MOM, :] for c, _ in chunks], axis=1)
                chan = chan.reshape(3, 16, len(chunks) * LANE)
                for j in range(WIN):
                    which = code_ref[w * WIN + j, first + i] & 255
                    if len(chunks) == NROW:
                        factor = table[which]
                    else:
                        factor = jnp.concatenate(
                            [table[which, :, pl.ds(pl.multiple_of(r * LANE, LANE), LANE)] for _, r in chunks], axis=1)
                    parts.append((chan * factor[None]).reshape(MOM, len(chunks) * LANE))
            scaled = jnp.concatenate(parts, axis=0)
            prod = lax.dot_general(scaled, win, (((1,), (1,)), ((), ())), preferred_element_type=F32)
            for i in range(HALF):
                acc = jnp.zeros((MOM, 256), F32)
                for j in range(WIN):
                    n = i * WIN + j
                    low = off + j * MOM
                    mine = prod[n * MOM:(n + 1) * MOM] * sign[code_ref[w * WIN + j, first + i] >> 8]
                    acc = jnp.where((lanes >= low) & (lanes < low + MOM), mine, acc)
                put(i, start, off, acc)

    def batch_rows(g, half):
        return pl.ds(pl.multiple_of((half * NB + g * HALF) * MOM, HROW), HROW)

    vsum[...] = jnp.zeros((2, HROW, 1024), F32)

    def own_part(p, carry):
        for k, fn in parts_before.items():
            pl.when(p == k)(fn)

        def place(k):
            d = (k + 1) // 2
            return lax.rem(jnp.where(lax.rem(k, 2) == 1, z + NZ - d, z + d), NZ)

        def one(half, carry_):
            chunks = []
            for k in (2 * p, 2 * p + 1):
                chunks.append((place(k), grid_part(half, place(k))))

            def put(i, start, off, acc):
                vsum[half, i * MOM:(i + 1) * MOM, start:start + 256] += acc

            products(x, half, chunks, put)
            return carry_

        return lax.fori_loop(0, 2, one, carry)

    lax.fori_loop(0, 4, own_part, 0)
    for half in range(2):
        vbuf[batch_rows(x, half), :] = vsum[half, :, 0:COLS].astype(BF)
        pown[half] = jnp.dot(vbuf[batch_rows(x, half), :], weighted[...], preferred_element_type=F32)

    def build(t, carry):
        for k, fn in befores.items():
            pl.when(t == k)(fn)
        d, g, half = batch(t)
        zs = lax.rem(2 * row + half, NZ)
        chunks = [(lax.rem(zs + shift(jnp.int32(r), row // 4), NZ), r) for r in range(NROW)]

        def put(i, start, off, acc):
            rows = pl.ds(pl.multiple_of((half * NB + g * HALF + i) * MOM, MOM), MOM)
            width = min(256, COLS - start)
            new = acc.astype(BF)
            if off:
                new = jnp.where(lanes >= off, new, vbuf[rows, start:start + width])
            vbuf[rows, start:start + width] = new[:, :width]

        products(g, half, chunks, put)
        part_sum = jnp.dot(vbuf[batch_rows(g, half), :], weighted[...], preferred_element_type=F32)
        psend[(d - 1) * 2 + half] = part_sum.astype(BF)
        p_copy(d, half).start()
        return carry

    lax.fori_loop(2, 8, build, 0)

    def tx_copy(d):
        to = lax.rem(x + d, NX)
        return copy(t16.at[pl.ds(to * NZ, NZ)], txrecv.at[d - 1], tx_s.at[d], tx_r.at[d], at_x(d))

    def second(operand):
        turned = operand.T.astype(BF)

        def chunk(q, carry):
            rows = pl.ds(pl.multiple_of(q * 384, 384), 384)
            prod = lax.dot_general(turned, vbuf[rows, :], (((1,), (1,)), ((), ())), preferred_element_type=F32)
            for jj in range(3):
                pbuf[jj] = prod[:, jj * LANE:(jj + 1) * LANE]
            for jj in range(3):
                for c in range(NX * NZ):
                    t32[c, pl.ds(q * 12 + jj * 4, 4), :] = pbuf[jj, 4 * c:4 * c + 4, :]
            return carry

        lax.fori_loop(0, 5, chunk, 0)
        t16[...] = t32[...].astype(BF)
        for d in (2, 1, 3):
            tx_copy(d).start()

    def turn(m, carry):
        at = pl.ds(pl.multiple_of(m * LANE, LANE), LANE)
        vturn[:, at] = vbuf[at, :].T
        return carry

    @pl.when(jnp.logical_not(in_slab))
    def _():
        second(weighted[...].astype(F32))

    for n in range(6):
        p_copy(n // 2 + 1, n % 2).wait_recv()
    for half in range(2):
        total = pown[half]
        for d in range(3):
            total = total + precv[d * 2 + half].astype(F32)
        ssum[half * PAD:half * PAD + HROW, :] = total
        zsend[half * PAD:half * PAD + HROW, :] = total.astype(BF)

    def shard(q):
        return pl.ds(pl.multiple_of(q * SH, SH), SH)

    def r_copy(d):
        return copy(zsend.at[shard(lax.rem(z + d, NZ))], zrecv.at[d - 1], r_s.at[d], r_r.at[d], at_z(d))

    for d in range(1, NZ):
        r_copy(d).start()
    lax.fori_loop(0, 4, turn, 0)
    for d in range(1, NZ):
        r_copy(d).wait_recv()
    total = bornp[shard(z), :] + ssum[shard(z), :]
    for d in range(NZ - 1):
        total = total + zrecv[d].astype(F32)
    fresh = total.astype(BF)
    fi[x, shard(z), :] = fresh
    yshard[y] = fresh

    def a_copy(d):
        return copy(yshard.at[y], yshard.at[y], a_s.at[d], a_r.at[d], at_y(d))

    for d in (2, 1, 3):
        a_copy(d).start()

    def u_copy(d):
        from_y = lax.rem(y + d, NY)
        return copy(yshard.at[from_y], upd.at[x, shard(lax.rem(z, 4))], u_s.at[d], u_r.at[x * 4 + lax.rem(z, 4)],
                    (row, use_col(from_y)))

    def u_self(d):
        return use_col(lax.rem(y + d, NY)) == col

    for d in (0, 1, 3, 2):
        if d > 0:
            from_y = lax.rem(y + d, NY)
            copy(yshard.at[from_y], yshard.at[from_y], a_s.at[d], a_r.at[NY - d], at_y(d)).wait_recv()

        @pl.when(u_self(d))
        def _():
            upd[x, shard(lax.rem(z, 4)), :] = yshard[lax.rem(y + d, NY)]

        @pl.when(jnp.logical_not(u_self(d)))
        def _():
            u_copy(d).start()

    def fz_copy(d):
        ref = fi.at[x, shard(z)]
        return copy(ref, ref, fz_s.at[d], fz_r.at[d], at_z(d))

    for d in range(1, NZ):
        fz_copy(d).start()

    def f_copy(g):
        ref = upd.at[g, pl.ds(0, HROW)]
        return copy(ref, ref, f_s.at[g], f_r.at[g], sibling)

    lax.fori_loop(4, 8, turn, 0)

    @pl.when(home)
    def _():
        for g in range(NX):
            for q in range(4):
                @pl.when(g * NZ + 4 * part + q != col)
                def _():
                    ref = upd.at[g, pl.ds(q * SH, SH)]
                    copy(ref, ref, u_s.at[0], u_r.at[g * 4 + q], sibling).wait_recv()
            f_copy(g).start()

    @pl.when(in_slab)
    def _():
        @pl.when(jnp.logical_not(home))
        def _():
            for g in range(NX):
                f_copy(g).wait_recv()
        fresh_rows = jnp.concatenate([upd[g, 0:HROW, :] for g in range(NX)], axis=0)
        second((gb_ref[...] * fresh_rows.astype(F32)).astype(BF).astype(F32))

    for d in range(1, NZ):
        ref = fi.at[x, shard(lax.rem(z + NZ - d, NZ))]
        copy(ref, ref, fz_s.at[d], fz_r.at[d], at_z(d)).wait_recv()

    def fx_copy(d, g):
        return copy(fi.at[g], fi.at[g], fx_s.at[d], fx_r.at[d], at_x(d))

    for d in (2, 1, 3):
        fx_copy(d, x).start()

    lax.fori_loop(8, 15, turn, 0)

    def v_copy():
        return pltpu.make_async_copy(vturn, v_out, out_s.at[8])

    v_copy().start()
    for j in range(15):
        bturn[j] = born_ref[j * LANE:(j + 1) * LANE, :].T

    for d in range(1, NX):
        tx_copy(d).wait_recv()
    total = t32[pl.ds(x * NZ, NZ)]
    for d in range(NX - 1):
        total = total + txrecv[d].astype(F32)
    tz32[...] = total
    tzsend[...] = total.astype(BF)

    def tz_copy(d):
        return copy(tzsend.at[lax.rem(z + d, NZ)], tzrecv.at[d - 1], tz_s.at[d], tz_r.at[d], at_z(d))

    for d in range(1, NZ):
        tz_copy(d).start()
    for d in range(1, NX):
        fx_copy(d, lax.rem(x + NX - d, NX)).wait_recv()

    def f_out(g, half):
        return pltpu.make_async_copy(fi.at[g, pl.ds(half * PAD, HROW)],
                                     first_out.at[pl.ds(half * COLS + g * HROW, HROW)], out_s.at[2 * g + half])

    for g in range(NX):
        for half in range(2):
            f_out(g, half).start()
    for d in range(1, NZ):
        tz_copy(d).wait_recv()
    total = tz32[z]
    for d in range(NZ - 1):
        total = total + tzrecv[d].astype(F32)
    tz32[z] = total
    for j in range(15):
        share_out[:, j * LANE:(j + 1) * LANE] = tz32[z, 4 * j:4 * j + 4, :] + bturn[j, pl.ds(4 * col, 4), :]

    for g in range(NX):
        for half in range(2):
            f_out(g, half).wait()
    v_copy().wait()

    @pl.when(in_slab)
    def _():
        for d in range(1, NX):
            s1_copy(d).wait_send()

    for xs in range(2):
        @pl.when(jnp.logical_not(s2_self(xs)))
        def _():
            s2_copy(xs).wait_send()
    for c in ys:
        c.wait_send()
    for f in (0, 1, 2, 4):
        for sign_ in (1, -1):
            for s in range(steps(f, sign_)):
                z_copy(f, sign_, s).wait_send()
    for k in range(8):
        xh2(k, 1).wait_send()
        xh2(k, -1).wait_send()
        xh2_forward(k).wait_send()
    for n in range(2):
        xh1(n).wait_send()
    for k in range(8):
        xf(k).wait_send()
    for n in range(6):
        p_copy(n // 2 + 1, n % 2).wait_send()
    for d in range(1, NZ):
        r_copy(d).wait_send()
        fz_copy(d).wait_send()
        tz_copy(d).wait_send()
    for d in range(1, NX):
        fx_copy(d, x).wait_send()
        tx_copy(d).wait_send()

    for d in range(1, NY):
        a_copy(d).wait_send()
    for d in range(NY):
        @pl.when(jnp.logical_not(u_self(d)))
        def _():
            u_copy(d).wait_send()

    @pl.when(home)
    def _():
        for g in range(NX):
            f_copy(g).wait_send()


def hand_over(v_in, f_in, s_in, v_out, f_out, s_out, v_mid, f_mid, s_mid, sem):
    trips = [(f_in, f_mid, f_out), (s_in, s_mid, s_out)]
    for q in range(6):
        rows = pl.ds(q * 160, 160)
        trips.append((v_in.at[rows], v_mid.at[rows], v_out.at[rows]))
    there = [pltpu.make_async_copy(src, mid, sem.at[n]) for n, (src, mid, _) in enumerate(trips)]
    back = [pltpu.make_async_copy(mid, dst, sem.at[8 + n]) for n, (_, mid, dst) in enumerate(trips)]
    for c in there:
        c.start()
    for c, d in zip(there, back):
        c.wait()
        d.start()
    for c in back:
        c.wait()


def body(radial, form_factors, coupling, quantum, green_diag, kmatrix, born_term):
    row_count, col_count = coupling.shape
    row_index, col_index = lax.axis_index("row"), lax.axis_index("col")
    rq = lax.dynamic_slice_in_dim(quantum, row_index * row_count, row_count, 0)
    cq = lax.dynamic_slice_in_dim(quantum, col_index * col_count, col_count, 0)
    table_index = coupling * (NTARG * NTARG) + rq[:, 2:3] * NTARG + cq[:, 2][None, :]
    parity = (rq[:, 0:1] + cq[:, 0][None, :]) % 2
    spread_m = jnp.abs(rq[:, 1:2] - cq[:, 1][None, :])
    code = (table_index + 256 * (4 * parity + spread_m)).T
    vm = pl.BlockSpec(memory_space=pltpu.VMEM)
    sm = pl.BlockSpec(memory_space=pltpu.SMEM)
    hb = pl.BlockSpec(memory_space=pl.ANY)
    dma = pltpu.SemaphoreType.DMA
    v_block, first, share = pl.pallas_call(
        kernel,
        out_shape=(
            jax.ShapeDtypeStruct((COLS, ROWS), BF),
            jax.ShapeDtypeStruct((ROWS, LANE), BF),
            jax.ShapeDtypeStruct((4, ROWS), F32),
        ),
        in_specs=[sm, vm, hb, vm, vm, hb],
        out_specs=(hb, hb, vm),
        scratch_shapes=[
            pltpu.SMEM((8,), F32),
            pltpu.VMEM((256, 16, GRID), BF),
            pltpu.VMEM((256, GRID), F32),
            pltpu.VMEM((NROW, 1024, LANE), BF),
            pltpu.VMEM((NX, 2, NROW, HROW, LANE), BF),
            pltpu.VMEM((2, HROW, LANE), BF),
            pltpu.VMEM((ROWS, COLS), BF),
            pltpu.VMEM((COLS, ROWS), BF),
            pltpu.VMEM((COLS, LANE), F32),
            pltpu.VMEM((COLS, LANE), BF),
            pltpu.VMEM((2, HROW, LANE), F32),
            pltpu.VMEM((6, HROW, LANE), BF),
            pltpu.VMEM((6, HROW, LANE), BF),
            pltpu.VMEM((2 * PAD, LANE), F32),
            pltpu.VMEM((2 * PAD, LANE), BF),
            pltpu.VMEM((NZ - 1, SH, LANE), BF),
            pltpu.VMEM((ROWS, LANE), F32),
            pltpu.VMEM((2 * PAD, LANE), F32),
            pltpu.VMEM((15, LANE, LANE), F32),
            pltpu.VMEM((2, HROW, 1024), F32),
            pltpu.VMEM((NX, 2 * PAD, LANE), BF),
            pltpu.VMEM((NY, SH, LANE), BF),
            pltpu.VMEM((NX, PAD, LANE), BF),
            pltpu.VMEM((NX * NZ, SH, LANE), F32),
            pltpu.VMEM((NX * NZ, SH, LANE), BF),
            pltpu.VMEM((3, LANE, LANE), F32),
            pltpu.VMEM((NX - 1, NZ, SH, LANE), BF),
            pltpu.VMEM((NZ, SH, LANE), F32),
            pltpu.VMEM((NZ, SH, LANE), BF),
            pltpu.VMEM((NZ - 1, SH, LANE), BF),
            dma((4,)), dma((2,)), dma((2,)), dma((2,)), dma((13,)), dma((13,)), dma((40,)), dma((40,)), dma((34,)), dma((34,)),
            dma((6,)), dma((6,)), dma((8,)), dma((8,)), dma((4,)), dma((4,)), dma((4,)), dma((16,)), dma((4,)), dma((4,)),
            dma((8,)), dma((8,)), dma((4,)), dma((4,)), dma((4,)), dma((4,)), dma((8,)), dma((8,)), dma((2,)), dma((9,)),
        ],
        compiler_params=pltpu.CompilerParams(collective_id=0, has_side_effects=True, vmem_limit_bytes=58 << 20),
        name="sweeps",
    )(code, radial.reshape(COLS, LANE), form_factors, green_diag, kmatrix, born_term)
    v_block, first, share = pl.pallas_call(
        hand_over,
        out_shape=(
            jax.ShapeDtypeStruct((COLS, ROWS), BF),
            jax.ShapeDtypeStruct((ROWS, LANE), BF),
            jax.ShapeDtypeStruct((4, ROWS), F32),
        ),
        in_specs=[hb, hb, hb],
        out_specs=(hb, hb, hb),
        scratch_shapes=[pltpu.VMEM((COLS, ROWS), BF), pltpu.VMEM((ROWS, LANE), BF), pltpu.VMEM((4, ROWS), F32), dma((16,))],
        name="hand_over",
    )(v_block, first, share)
    return v_block.T, first, share.T


def solution(mesh):
    placed = (
        P("col", None, "row"),
        P(),
        P("row", "col"),
        P(),
        P("col", None),
        P("col", None),
        P("row", None),
    )
    return jax.shard_map(
        body,
        mesh=mesh,
        in_specs=placed,
        out_specs=(P("row", "col"), P("row", None), P("row", "col")),
        check_vma=False,
    )
```

```python
import functools

import jax
import jax.numpy as jnp
from jax import lax
from jax.experimental import pallas as pl
from jax.experimental.pallas import tpu as pltpu
from jax.sharding import PartitionSpec as P

NTARG = 4
MESH = pl.DeviceIdType.MESH
BF, F32 = jnp.bfloat16, jnp.float32

NX, NZ, NY = 4, 8, 4
NROW = 8
MOM = 48
GRID = 1024
LANE = 128
NB = 20
HALF = 5
HROW = HALF * MOM
COLS = NB * MOM
MID = COLS // 2
ROWS = 2 * COLS
SH = 64
PAD = 4 * SH
WIN = 4
NWIN = NB // WIN


def kernel(code_ref, rad_ref, form_hbm, green_ref, kmat_ref, born_hbm,
           v_out, first_out, share_out,
           sign, table, form_ref, colp, rowp, mid, vbuf, vturn, gb_ref, weighted, pown, psend, precv, ssum, zsend, zrecv,
           born_ref, bornp, bturn, vsum, fi, yshard, upd, t32, t16, pbuf, txrecv, tz32, tzsend, tzrecv,
           s1_s, s1_r, s2_s, s2_r, y_s, y_r, z_s, z_r, x_s, x_r, p_s, p_r, r_s, r_r, a_s, a_r, u_s, u_r, f_s, f_r,
           fz_s, fz_r, fx_s, fx_r, tx_s, tx_r, tz_s, tz_r, in_s, out_s):
    row = lax.axis_index("row")
    col = lax.axis_index("col")
    x, z = col // NZ, col % NZ
    y, core = row // 2, row % 2

    def at_x(d):
        return (row, lax.rem(x + d, NX) * NZ + z)

    def at_z(d):
        return (row, x * NZ + lax.rem(z + d, NZ))

    def at_y(d):
        return (lax.rem(y + d, NY) * 2 + core, col)

    sibling = (y * 2 + 1 - core, col)
    in_slab = col < 2 * NROW

    def shift(r, xs):
        k = lax.rem(r // 2 + 2 * xs, 4)
        return jnp.where(lax.rem(r, 2) == 0, k, jnp.where(k == 0, 4, 8 - k))

    def s2_to(xs):
        return 4 * xs + z // 2, lax.rem(z + shift(row, xs), NZ)

    def s2_self(xs):
        to_row, to_z = s2_to(xs)
        return (to_row == row) & (to_z == z)

    def s2_from(half):
        xs, zs = row // 4, lax.rem(2 * row + half, NZ)
        s = lax.rem(z - zs + NZ, NZ)
        k = lax.rem(jnp.minimum(s, NZ - s) + 2 * xs, 4)
        return 2 * k + (s >= 4).astype(jnp.int32), zs

    def s2_from_self(half):
        r, zs = s2_from(half)
        return (r == row) & (zs == z)

    part = col % 2

    def use_col(from_y):
        return from_y // 2 * NZ + 4 * lax.rem(from_y, 2) + 2 * core + z // 4

    home = in_slab & ((col // 2) % 2 == core)

    def copy(src, dst, ss, rs, dev):
        return pltpu.make_async_remote_copy(src_ref=src, dst_ref=dst, send_sem=ss, recv_sem=rs,
                                            device_id=dev, device_id_type=MESH)

    loads = [pltpu.make_async_copy(form_hbm, form_ref, in_s.at[0]), pltpu.make_async_copy(born_hbm, born_ref, in_s.at[1])]
    for c in loads:
        c.start()

    bar = pltpu.get_barrier_semaphore()

    def greet(dev):
        pl.semaphore_signal(bar, inc=1, device_id=dev, device_id_type=MESH)

    for d in range(1, NZ):
        greet(at_z(d))
    for d in range(1, NX):
        greet(at_x(d))
    for d in range(1, NY):
        greet(at_y(d))
    greet(sibling)
    for half in range(2):
        @pl.when(jnp.logical_not(s2_from_self(half)))
        def _():
            r, zs = s2_from(half)
            greet((r, x * NZ + zs))

    @pl.when(home)
    def _():
        def hello(k, carry):
            xx, zz = k // 4, 4 * part + lax.rem(k, 4)

            @pl.when(xx * NZ + zz != col)
            def _():
                greet((row, xx * NZ + zz))
            return carry

        lax.fori_loop(0, 16, hello, 0)

    n_wait = 7 + 3 + 3 + 1 + 4 + 2
    for from_y in range(NY):
        n_wait = n_wait - (use_col(from_y) == col).astype(jnp.int32)
    for xs in range(2):
        n_wait = n_wait - s2_self(xs).astype(jnp.int32)
    pl.semaphore_wait(bar, n_wait)

    def s1_copy(d):
        g = lax.rem(x + d, NX)
        src = rad_ref.at[pl.ds(pl.multiple_of(g * HROW, HROW), HROW)]
        return copy(src, mid.at[x], s1_s.at[d], s1_r.at[x], at_x(d))

    @pl.when(in_slab)
    def _():
        for d in (2, 1, 3):
            s1_copy(d).start()
        mid[x] = rad_ref[pl.ds(pl.multiple_of(x * HROW, HROW), HROW), :]

    below, above = lax.rem(y + 3, NY) * 2 + core, lax.rem(y + 1, NY) * 2 + core
    across = lax.rem(y + 2, NY) * 2 + core
    lo, hi = pl.ds(0, MID), pl.ds(MID, MID)

    def y_copy(k, src, dst, dev):
        return copy(src, dst, y_s.at[k], y_r.at[k], dev)

    def y_part(k, r, part_, dev):
        return y_copy(k, colp.at[r, part_], colp.at[r, part_], dev)

    ys = [
        y_copy(0, rad_ref.at[lo], colp.at[row, lo], at_y(1)),
        y_copy(1, rad_ref.at[hi], colp.at[row, hi], at_y(3)),
        y_copy(2, rad_ref.at[hi], colp.at[row, hi], at_y(1)),
        y_copy(3, rad_ref.at[lo], colp.at[row, lo], at_y(3)),
        y_copy(4, rad_ref, colp.at[row, pl.ds(0, COLS)], sibling),
        y_part(5, below, lo, at_y(1)),
        y_part(6, above, hi, at_y(3)),
        y_part(7, below, lo, sibling),
        y_part(8, above, hi, sibling),
        y_part(9, below, hi, sibling),
        y_part(10, above, lo, sibling),
        y_part(11, across, lo, sibling),
        y_part(12, across, hi, sibling),
    ]
    for k in range(5):
        ys[k].start()
    colp[row, 0:COLS, :] = rad_ref[...]

    def spread(i, carry):
        table[i] = jnp.broadcast_to(form_ref[pl.ds(i, 1), :], (16, GRID)).astype(BF)
        return carry

    loads[0].wait()
    lax.fori_loop(0, 64, spread, 0, unroll=4)

    def s2_copy(xs):
        to_row, to_z = s2_to(xs)
        half = lax.rem(z, 2)
        return copy(mid.at[xs], rowp.at[x, half, to_z], s2_s.at[xs], s2_r.at[half], (to_row, x * NZ + to_z))

    def s2_start(xs):
        @pl.when(s2_self(xs))
        def _():
            rowp[x, lax.rem(z, 2), z] = mid[xs]

        @pl.when(jnp.logical_not(s2_self(xs)))
        def _():
            s2_copy(xs).start()

    @pl.when(in_slab)
    def _():
        s2_start(x)

    for xs in range(2):
        @pl.when(x != xs)
        def _():
            copy(mid.at[xs], mid.at[xs], s1_s.at[0], s1_r.at[xs], sibling).wait_recv()
            s2_start(xs)

    for k in range(8):
        sign[k] = jnp.float32((1.0 - 2.0 * (k // 4)) / (1.0 + k % 4))
    colp[:, COLS:, :] = jnp.zeros((NROW, 1024 - COLS, LANE), BF)
    for half in range(2):
        edge = slice(half * PAD + HROW, (half + 1) * PAD)
        zsend[edge, :] = jnp.zeros((PAD - HROW, LANE), BF)
        ssum[edge, :] = jnp.zeros((PAD - HROW, LANE), F32)
        bornp[edge, :] = jnp.zeros((PAD - HROW, LANE), F32)
    t32[:, 60:, :] = jnp.zeros((NX * NZ, 4, LANE), F32)

    for b in range(NB):
        gb_ref[b * MOM:(b + 1) * MOM, :] = jnp.broadcast_to(green_ref[b:b + 1, :], (LANE, MOM)).T
    weighted[...] = (gb_ref[...] * kmat_ref[...].astype(F32)).astype(BF)

    lax.fori_loop(64, 128, spread, 0, unroll=4)

    def flow_at(f):
        if f == 0:
            return x, 0
        return lax.rem(x + f - 1, NX), 1

    def steps(f, sign):
        return 4 if (f in (0, 2)) == (sign > 0) else 3

    def z_copy(f, sign, s):
        g, half = flow_at(f)
        origin = lax.rem(z + (NZ - s if sign > 0 else s), NZ)
        k = (f * 2 + (0 if sign > 0 else 1)) * 4 + s
        ref = rowp.at[g, half, origin]
        return copy(ref, ref, z_s.at[k], z_r.at[k], at_z(1 if sign > 0 else NZ - 1))

    def z_wait(f, sign, s):
        z_copy(f, sign, s).wait_recv()
        if s + 1 < steps(f, sign):
            z_copy(f, sign, s + 1).start()

    def piece(k):
        d = (k + 1) // 2
        return lax.rem(z + (NZ - d if k % 2 == 1 else d), NZ)

    def xh2(k, sign):
        ref = rowp.at[x, 0, piece(k)]
        n = k if sign > 0 else 8 + k
        return copy(ref, ref, x_s.at[n], x_r.at[n], at_x(1 if sign > 0 else 3))

    def xh2_forward(k):
        sign = 1 if k % 2 == 0 else -1
        ref = rowp.at[lax.rem(x + (3 if sign > 0 else 1), NX), 0, piece(k)]
        return copy(ref, ref, x_s.at[16 + k], x_r.at[16 + k], at_x(1 if sign > 0 else 3))

    def xh2_start(k):
        xh2(k, 1).start()
        xh2(k, -1).start()

    def xh2_wait(k):
        xh2(k, 1).wait_recv()
        xh2(k, -1).wait_recv()

    def xh1(n):
        ref = rowp.at[x, 1, z]
        return copy(ref, ref, x_s.at[24 + n], x_r.at[24 + n], at_x(3 if n == 1 else 1))

    def xf(k):
        sign = 1 if k % 2 == 0 else -1
        ref = rowp.at[lax.rem(x + (3 if sign > 0 else 1), NX), 1, piece(k)]
        return copy(ref, ref, x_s.at[26 + k], x_r.at[26 + k], at_x(1 if sign > 0 else 3))

    def flow_start(f):
        z_copy(f, 1, 0).start()
        z_copy(f, -1, 0).start()

    def sc_wait(half):
        @pl.when(jnp.logical_not(s2_from_self(half)))
        def _():
            ref = rowp.at[x, half, z]
            copy(ref, ref, s2_s.at[0], s2_r.at[half], sibling).wait_recv()

    sc_wait(0)
    flow_start(0)
    xh2_start(0)
    sc_wait(1)
    flow_start(1)
    xh1(0).start()
    xh1(1).start()

    def y_on(k, *then):
        ys[k].wait_recv()
        for n in then:
            ys[n].start()

    y_on(0, 5, 7)
    y_on(1, 6, 8)
    lax.fori_loop(128, 192, spread, 0, unroll=4)
    y_on(2, 9)
    y_on(3, 10)

    def own_step(s_):
        for sign_ in (1, -1):
            if s_ < steps(0, sign_):
                z_wait(0, sign_, s_)
                xh2_start(2 * s_ + (1 if sign_ > 0 else 2))
        for sign_ in (1, -1):
            if s_ < steps(1, sign_):
                z_wait(1, sign_, s_)

    def far_step(s_):
        if s_ < 3:
            z_wait(4, 1, s_)
        z_wait(4, -1, s_)
        if s_ < 3:
            xf(2 * s_ + 2).start()
        z_wait(2, 1, s_)
        xf(2 * s_ + 1).start()
        if s_ < 3:
            z_wait(2, -1, s_)

    def part_0():
        own_step(0)
        lax.fori_loop(192, 256, spread, 0, unroll=4)
        y_on(5, 11)
        y_on(6, 12)
        xh1(0).wait_recv()
        xf(0).start()
        flow_start(4)
        xh1(1).wait_recv()
        flow_start(2)
        xh2_wait(0)
        for k in (4, 7, 8, 9, 10, 11, 12):
            ys[k].wait_recv()

    def part_1():
        own_step(1)
        far_step(0)
        xh2_wait(1)
        xh2_wait(2)

    def part_2():
        own_step(2)
        xh2_wait(3)
        xh2_wait(4)
        for k in range(3):
            xh2_forward(k).start()
        loads[1].wait()
        for half in range(2):
            bornp[half * PAD:half * PAD + HROW, :] = born_ref[pl.ds(pl.multiple_of(half * COLS + x * HROW, HROW), HROW), :]

    def part_3():
        own_step(3)
        far_step(1)
        xh2_wait(5)
        xh2_wait(6)
        for k in range(3, 7):
            xh2_forward(k).start()

    def before_2():
        xh2_wait(7)
        xh2_forward(7).start()

    def before_3():
        far_step(2)

    def before_4():
        for k in range(8):
            xh2_forward(k).wait_recv()

    def before_5():
        far_step(3)

    def before_6():
        pass

    def before_7():
        for k in range(8):
            xf(k).wait_recv()

    parts_before = {0: part_0, 1: part_1, 2: part_2, 3: part_3}
    befores = {2: before_2, 3: before_3, 4: before_4, 5: before_5, 6: before_6, 7: before_7}

    def p_copy(d, half):
        n = (d - 1) * 2 + half
        return copy(psend.at[n], precv.at[n], p_s.at[n], p_r.at[n], at_x(d))

    def batch(t):
        third = lax.rem(t - 2, 3)
        d = jnp.where(third == 0, 1, jnp.where(third == 1, 3, 2))
        half = jnp.where(t >= 5, 1, 0)
        return d, lax.rem(x + d, NX), half

    lanes = lax.broadcasted_iota(jnp.int32, (MOM, 256), 1)

    def grid_part(half, slot_):
        step = lax.rem(slot_ - lax.rem(2 * row + half, NZ) + NZ, NZ)
        k = lax.rem(jnp.minimum(step, NZ - step) + 2 * (row // 4), 4)
        return 2 * k + (step >= 4).astype(jnp.int32)

    def products(g, half, chunks, put):
        first = half * NB + g * HALF
        for w in range(NWIN):
            base = w * WIN * MOM
            start = base // LANE * LANE
            off = base - start
            win = jnp.concatenate([colp[r, start:start + 256, :] for _, r in chunks], axis=1)
            parts = []
            for i in range(HALF):
                chan = jnp.concatenate([rowp[g, half, c, i * MOM:(i + 1) * MOM, :] for c, _ in chunks], axis=1)
                chan = chan.reshape(3, 16, len(chunks) * LANE)
                for j in range(WIN):
                    which = code_ref[w * WIN + j, first + i] & 255
                    if len(chunks) == NROW:
                        factor = table[which]
                    else:
                        factor = jnp.concatenate(
                            [table[which, :, pl.ds(pl.multiple_of(r * LANE, LANE), LANE)] for _, r in chunks], axis=1)
                    parts.append((chan * factor[None]).reshape(MOM, len(chunks) * LANE))
            scaled = jnp.concatenate(parts, axis=0)
            prod = lax.dot_general(scaled, win, (((1,), (1,)), ((), ())), preferred_element_type=F32)
            for i in range(HALF):
                acc = jnp.zeros((MOM, 256), F32)
                for j in range(WIN):
                    n = i * WIN + j
                    low = off + j * MOM
                    mine = prod[n * MOM:(n + 1) * MOM] * sign[code_ref[w * WIN + j, first + i] >> 8]
                    acc = jnp.where((lanes >= low) & (lanes < low + MOM), mine, acc)
                put(i, start, off, acc)

    def batch_rows(g, half):
        return pl.ds(pl.multiple_of((half * NB + g * HALF) * MOM, HROW), HROW)

    vsum[...] = jnp.zeros((2, HROW, 1024), F32)

    def own_part(p, carry):
        for k, fn in parts_before.items():
            pl.when(p == k)(fn)

        def place(k):
            d = (k + 1) // 2
            return lax.rem(jnp.where(lax.rem(k, 2) == 1, z + NZ - d, z + d), NZ)

        def one(half, carry_):
            chunks = []
            for k in (2 * p, 2 * p + 1):
                chunks.append((place(k), grid_part(half, place(k))))

            def put(i, start, off, acc):
                vsum[half, i * MOM:(i + 1) * MOM, start:start + 256] += acc

            products(x, half, chunks, put)
            return carry_

        return lax.fori_loop(0, 2, one, carry)

    lax.fori_loop(0, 4, own_part, 0)
    for half in range(2):
        vbuf[batch_rows(x, half), :] = vsum[half, :, 0:COLS].astype(BF)
        pown[half] = jnp.dot(vbuf[batch_rows(x, half), :], weighted[...], preferred_element_type=F32)

    def build(t, carry):
        for k, fn in befores.items():
            pl.when(t == k)(fn)
        d, g, half = batch(t)
        zs = lax.rem(2 * row + half, NZ)
        chunks = [(lax.rem(zs + shift(jnp.int32(r), row // 4), NZ), r) for r in range(NROW)]

        def put(i, start, off, acc):
            rows = pl.ds(pl.multiple_of((half * NB + g * HALF + i) * MOM, MOM), MOM)
            width = min(256, COLS - start)
            new = acc.astype(BF)
            if off:
                new = jnp.where(lanes >= off, new, vbuf[rows, start:start + width])
            vbuf[rows, start:start + width] = new[:, :width]

        products(g, half, chunks, put)
        part_sum = jnp.dot(vbuf[batch_rows(g, half), :], weighted[...], preferred_element_type=F32)
        psend[(d - 1) * 2 + half] = part_sum.astype(BF)
        p_copy(d, half).start()
        return carry

    lax.fori_loop(2, 8, build, 0)

    def tx_copy(d):
        to = lax.rem(x + d, NX)
        return copy(t16.at[pl.ds(to * NZ, NZ)], txrecv.at[d - 1], tx_s.at[d], tx_r.at[d], at_x(d))

    def second(operand):
        turned = operand.T.astype(BF)

        def chunk(q, carry):
            rows = pl.ds(pl.multiple_of(q * 384, 384), 384)
            prod = lax.dot_general(turned, vbuf[rows, :], (((1,), (1,)), ((), ())), preferred_element_type=F32)
            for jj in range(3):
                pbuf[jj] = prod[:, jj * LANE:(jj + 1) * LANE]
            for jj in range(3):
                for c in range(NX * NZ):
                    t32[c, pl.ds(q * 12 + jj * 4, 4), :] = pbuf[jj, 4 * c:4 * c + 4, :]
            return carry

        lax.fori_loop(0, 5, chunk, 0)
        t16[...] = t32[...].astype(BF)
        for d in (2, 1, 3):
            tx_copy(d).start()

    def turn(m, carry):
        at = pl.ds(pl.multiple_of(m * LANE, LANE), LANE)
        vturn[:, at] = vbuf[at, :].T
        return carry

    @pl.when(jnp.logical_not(in_slab))
    def _():
        second(weighted[...].astype(F32))

    for n in range(6):
        p_copy(n // 2 + 1, n % 2).wait_recv()
    for half in range(2):
        total = pown[half]
        for d in range(3):
            total = total + precv[d * 2 + half].astype(F32)
        ssum[half * PAD:half * PAD + HROW, :] = total
        zsend[half * PAD:half * PAD + HROW, :] = total.astype(BF)

    def shard(q):
        return pl.ds(pl.multiple_of(q * SH, SH), SH)

    def r_copy(d):
        return copy(zsend.at[shard(lax.rem(z + d, NZ))], zrecv.at[d - 1], r_s.at[d], r_r.at[d], at_z(d))

    for d in range(1, NZ):
        r_copy(d).start()
    lax.fori_loop(0, 4, turn, 0)
    for d in range(1, NZ):
        r_copy(d).wait_recv()
    total = bornp[shard(z), :] + ssum[shard(z), :]
    for d in range(NZ - 1):
        total = total + zrecv[d].astype(F32)
    fresh = total.astype(BF)
    fi[x, shard(z), :] = fresh
    yshard[y] = fresh

    def a_copy(d):
        return copy(yshard.at[y], yshard.at[y], a_s.at[d], a_r.at[d], at_y(d))

    for d in (2, 1, 3):
        a_copy(d).start()

    def u_copy(d):
        from_y = lax.rem(y + d, NY)
        return copy(yshard.at[from_y], upd.at[x, shard(lax.rem(z, 4))], u_s.at[d], u_r.at[x * 4 + lax.rem(z, 4)],
                    (row, use_col(from_y)))

    def u_self(d):
        return use_col(lax.rem(y + d, NY)) == col

    for d in (0, 1, 3, 2):
        if d > 0:
            from_y = lax.rem(y + d, NY)
            copy(yshard.at[from_y], yshard.at[from_y], a_s.at[d], a_r.at[NY - d], at_y(d)).wait_recv()

        @pl.when(u_self(d))
        def _():
            upd[x, shard(lax.rem(z, 4)), :] = yshard[lax.rem(y + d, NY)]

        @pl.when(jnp.logical_not(u_self(d)))
        def _():
            u_copy(d).start()

    def fz_copy(d):
        ref = fi.at[x, shard(z)]
        return copy(ref, ref, fz_s.at[d], fz_r.at[d], at_z(d))

    for d in range(1, NZ):
        fz_copy(d).start()

    def f_copy(g):
        ref = upd.at[g, pl.ds(0, HROW)]
        return copy(ref, ref, f_s.at[g], f_r.at[g], sibling)

    lax.fori_loop(4, 8, turn, 0)

    @pl.when(home)
    def _():
        for g in range(NX):
            for q in range(4):
                @pl.when(g * NZ + 4 * part + q != col)
                def _():
                    ref = upd.at[g, pl.ds(q * SH, SH)]
                    copy(ref, ref, u_s.at[0], u_r.at[g * 4 + q], sibling).wait_recv()
            f_copy(g).start()

    @pl.when(in_slab)
    def _():
        @pl.when(jnp.logical_not(home))
        def _():
            for g in range(NX):
                f_copy(g).wait_recv()
        fresh_rows = jnp.concatenate([upd[g, 0:HROW, :] for g in range(NX)], axis=0)
        second((gb_ref[...] * fresh_rows.astype(F32)).astype(BF).astype(F32))

    for d in range(1, NZ):
        ref = fi.at[x, shard(lax.rem(z + NZ - d, NZ))]
        copy(ref, ref, fz_s.at[d], fz_r.at[d], at_z(d)).wait_recv()

    def fx_copy(d, g):
        return copy(fi.at[g], fi.at[g], fx_s.at[d], fx_r.at[d], at_x(d))

    for d in (2, 1, 3):
        fx_copy(d, x).start()

    lax.fori_loop(8, 15, turn, 0)

    def v_copy():
        return pltpu.make_async_copy(vturn, v_out, out_s.at[8])

    v_copy().start()
    for j in range(15):
        bturn[j] = born_ref[j * LANE:(j + 1) * LANE, :].T

    for d in range(1, NX):
        tx_copy(d).wait_recv()
    total = t32[pl.ds(x * NZ, NZ)]
    for d in range(NX - 1):
        total = total + txrecv[d].astype(F32)
    tz32[...] = total
    tzsend[...] = total.astype(BF)

    def tz_copy(d):
        return copy(tzsend.at[lax.rem(z + d, NZ)], tzrecv.at[d - 1], tz_s.at[d], tz_r.at[d], at_z(d))

    for d in range(1, NZ):
        tz_copy(d).start()
    for d in range(1, NX):
        fx_copy(d, lax.rem(x + NX - d, NX)).wait_recv()

    def f_out(g, half):
        return pltpu.make_async_copy(fi.at[g, pl.ds(half * PAD, HROW)],
                                     first_out.at[pl.ds(half * COLS + g * HROW, HROW)], out_s.at[2 * g + half])

    for g in range(NX):
        for half in range(2):
            f_out(g, half).start()
    for d in range(1, NZ):
        tz_copy(d).wait_recv()
    total = tz32[z]
    for d in range(NZ - 1):
        total = total + tzrecv[d].astype(F32)
    tz32[z] = total
    for j in range(15):
        share_out[:, j * LANE:(j + 1) * LANE] = tz32[z, 4 * j:4 * j + 4, :] + bturn[j, pl.ds(4 * col, 4), :]

    for g in range(NX):
        for half in range(2):
            f_out(g, half).wait()
    v_copy().wait()

    @pl.when(in_slab)
    def _():
        for d in range(1, NX):
            s1_copy(d).wait_send()

    for xs in range(2):
        @pl.when(jnp.logical_not(s2_self(xs)))
        def _():
            s2_copy(xs).wait_send()
    for c in ys:
        c.wait_send()
    for f in (0, 1, 2, 4):
        for sign_ in (1, -1):
            for s in range(steps(f, sign_)):
                z_copy(f, sign_, s).wait_send()
    for k in range(8):
        xh2(k, 1).wait_send()
        xh2(k, -1).wait_send()
        xh2_forward(k).wait_send()
    for n in range(2):
        xh1(n).wait_send()
    for k in range(8):
        xf(k).wait_send()
    for n in range(6):
        p_copy(n // 2 + 1, n % 2).wait_send()
    for d in range(1, NZ):
        r_copy(d).wait_send()
        fz_copy(d).wait_send()
        tz_copy(d).wait_send()
    for d in range(1, NX):
        fx_copy(d, x).wait_send()
        tx_copy(d).wait_send()

    for d in range(1, NY):
        a_copy(d).wait_send()
    for d in range(NY):
        @pl.when(jnp.logical_not(u_self(d)))
        def _():
            u_copy(d).wait_send()

    @pl.when(home)
    def _():
        for g in range(NX):
            f_copy(g).wait_send()


def hand_over(v_in, f_in, s_in, v_out, f_out, s_out, v_mid, f_mid, s_mid, sem):
    trips = [(f_in, f_mid, f_out), (s_in, s_mid, s_out)]
    for q in range(6):
        rows = pl.ds(q * 160, 160)
        trips.append((v_in.at[rows], v_mid.at[rows], v_out.at[rows]))
    there = [pltpu.make_async_copy(src, mid, sem.at[n]) for n, (src, mid, _) in enumerate(trips)]
    back = [pltpu.make_async_copy(mid, dst, sem.at[8 + n]) for n, (_, mid, dst) in enumerate(trips)]
    for c in there:
        c.start()
    for c, d in zip(there, back):
        c.wait()
        d.start()
    for c in back:
        c.wait()


def body(radial, form_factors, coupling, quantum, green_diag, kmatrix, born_term):
    row_count, col_count = coupling.shape
    row_index, col_index = lax.axis_index("row"), lax.axis_index("col")
    rq = lax.dynamic_slice_in_dim(quantum, row_index * row_count, row_count, 0)
    cq = lax.dynamic_slice_in_dim(quantum, col_index * col_count, col_count, 0)
    table_index = coupling * (NTARG * NTARG) + rq[:, 2:3] * NTARG + cq[:, 2][None, :]
    parity = (rq[:, 0:1] + cq[:, 0][None, :]) % 2
    spread_m = jnp.abs(rq[:, 1:2] - cq[:, 1][None, :])
    code = (table_index + 256 * (4 * parity + spread_m)).T
    vm = pl.BlockSpec(memory_space=pltpu.VMEM)
    sm = pl.BlockSpec(memory_space=pltpu.SMEM)
    hb = pl.BlockSpec(memory_space=pl.ANY)
    dma = pltpu.SemaphoreType.DMA
    v_block, first, share = pl.pallas_call(
        kernel,
        out_shape=(
            jax.ShapeDtypeStruct((COLS, ROWS), BF),
            jax.ShapeDtypeStruct((ROWS, LANE), BF),
            jax.ShapeDtypeStruct((4, ROWS), F32),
        ),
        in_specs=[sm, vm, hb, vm, vm, hb],
        out_specs=(hb, hb, vm),
        scratch_shapes=[
            pltpu.SMEM((8,), F32),
            pltpu.VMEM((256, 16, GRID), BF),
            pltpu.VMEM((256, GRID), F32),
            pltpu.VMEM((NROW, 1024, LANE), BF),
            pltpu.VMEM((NX, 2, NROW, HROW, LANE), BF),
            pltpu.VMEM((2, HROW, LANE), BF),
            pltpu.VMEM((ROWS, COLS), BF),
            pltpu.VMEM((COLS, ROWS), BF),
            pltpu.VMEM((COLS, LANE), F32),
            pltpu.VMEM((COLS, LANE), BF),
            pltpu.VMEM((2, HROW, LANE), F32),
            pltpu.VMEM((6, HROW, LANE), BF),
            pltpu.VMEM((6, HROW, LANE), BF),
            pltpu.VMEM((2 * PAD, LANE), F32),
            pltpu.VMEM((2 * PAD, LANE), BF),
            pltpu.VMEM((NZ - 1, SH, LANE), BF),
            pltpu.VMEM((ROWS, LANE), F32),
            pltpu.VMEM((2 * PAD, LANE), F32),
            pltpu.VMEM((15, LANE, LANE), F32),
            pltpu.VMEM((2, HROW, 1024), F32),
            pltpu.VMEM((NX, 2 * PAD, LANE), BF),
            pltpu.VMEM((NY, SH, LANE), BF),
            pltpu.VMEM((NX, PAD, LANE), BF),
            pltpu.VMEM((NX * NZ, SH, LANE), F32),
            pltpu.VMEM((NX * NZ, SH, LANE), BF),
            pltpu.VMEM((3, LANE, LANE), F32),
            pltpu.VMEM((NX - 1, NZ, SH, LANE), BF),
            pltpu.VMEM((NZ, SH, LANE), F32),
            pltpu.VMEM((NZ, SH, LANE), BF),
            pltpu.VMEM((NZ - 1, SH, LANE), BF),
            dma((4,)), dma((2,)), dma((2,)), dma((2,)), dma((13,)), dma((13,)), dma((40,)), dma((40,)), dma((34,)), dma((34,)),
            dma((6,)), dma((6,)), dma((8,)), dma((8,)), dma((4,)), dma((4,)), dma((4,)), dma((16,)), dma((4,)), dma((4,)),
            dma((8,)), dma((8,)), dma((4,)), dma((4,)), dma((4,)), dma((4,)), dma((8,)), dma((8,)), dma((2,)), dma((9,)),
        ],
        compiler_params=pltpu.CompilerParams(collective_id=0, has_side_effects=True, vmem_limit_bytes=58 << 20),
        name="sweeps",
    )(code, radial.reshape(COLS, LANE), form_factors, green_diag, kmatrix, born_term)
    v_block, first, share = pl.pallas_call(
        hand_over,
        out_shape=(
            jax.ShapeDtypeStruct((COLS, ROWS), BF),
            jax.ShapeDtypeStruct((ROWS, LANE), BF),
            jax.ShapeDtypeStruct((4, ROWS), F32),
        ),
        in_specs=[hb, hb, hb],
        out_specs=(hb, hb, hb),
        scratch_shapes=[pltpu.VMEM((COLS, ROWS), BF), pltpu.VMEM((ROWS, LANE), BF), pltpu.VMEM((4, ROWS), F32), dma((16,))],
        name="hand_over",
    )(v_block, first, share)
    return v_block.T, first, share.T


def solution(mesh):
    placed = (
        P("col", None, "row"),
        P(),
        P("row", "col"),
        P(),
        P("col", None),
        P("col", None),
        P("row", None),
    )
    return jax.shard_map(
        body,
        mesh=mesh,
        in_specs=placed,
        out_specs=(P("row", "col"), P("row", None), P("row", "col")),
        check_vma=False,
    )
```
